32 devices in a mesh: groups: 2 (over x), gx: 16 (over z, y, core).
Axes of the slice: x: 2, y: 2, z: 4, core: 2. Of those that a mesh axis runs over, the one named last changes fastest.
Arguments:
- counts: int32 [32], P('groups'), parts along dimension 0, may hold values from 4 to 12, as said below
- resid: float32 [3, 512, 1024], P(None, ('groups', 'gx')), parts along dimension 1, may hold values from -6 to 6
- accum: float32 [9, 512, 1024], P(None, ('groups', 'gx')), parts along dimension 1
- mobility: float32 [9, 512, 1024], P(None, ('groups', 'gx')), parts along dimension 1
- trans: float32 [3, 512, 1024], P(None, ('groups', 'gx')), parts along dimension 1, may hold values from 0.02 to 1
- decouple: float32 [2, 512, 1024], P(None, ('groups', 'gx')), parts along dimension 1, may hold values from 0.3 to 1
Outputs:
- correction: float32 [3, 512, 1024], P(None, ('groups', 'gx')), parts along dimension 1
The draws below stay inside these ranges and needn't reach their ends.
There are 2 independent parts, one for each index of `groups`. The reference program is written for one: setup_inputs(seed, part) draws one part's arguments, and reference() takes and returns one part's arrays. A program takes and returns all parts, laid end to end along the dimension named above; each array names one. Nothing has to cross between parts.
Inputs may be any that keep to these rules, and one draw needn't show every extreme that they name: Partition p holds the planes from s_p = counts[0] + ... + counts[p-1] on; s_p - p * 8 lies between -(2) and 2, both ends taken at two neighbouring partitions in every draw, and the counts sum to 128.
All inputs are finite; a program needn't handle non-finite values.
Results may differ from the reference program's by a relative error of at most 0.0003.
Values sent between devices are 32-bit elements; how exact they have to be, the bound alone decides.
A program may use at most 64 MiB of HBM per device.

```python
import jax
import jax.numpy as jnp
from jax import lax

CX = 8
NY = 32
NZ = 32
CHEB = 6
SWEEPS = 6
CAP = 16
NX = 128
N_GX = 16


def draw_counts(key, part):
    key = jax.random.fold_in(key, 5)
    rim_planes = CX // 2 - 2
    key_drift, key_peak = jax.random.split(key)
    drift_values = jax.random.randint(key_drift, (N_GX + 1,), -rim_planes, rim_planes + 1)
    peak_index = jax.random.randint(key_peak, (), 1, N_GX - 1)
    drift_values = drift_values.at[0].set(0).at[N_GX].set(0)
    drift_values = drift_values.at[peak_index].set(-rim_planes).at[peak_index + 1].set(rim_planes)
    return (CX + drift_values[1:] - drift_values[:-1]).astype(jnp.int32)


def draw_accum(key, part):
    key = jax.random.fold_in(key, 7)
    key_scale, key_mixing = jax.random.split(key)
    cells = (N_GX * 2 * CX, NY * NZ)
    spread_draw = jax.random.uniform(key_scale, (3,) + cells, jnp.float32)
    scales = 0.01 * jnp.exp(jnp.log(10.0) * spread_draw)
    mixing = jax.random.uniform(key_mixing, (9,) + cells, jnp.float32, -0.2, 0.2)
    entries = []
    for row_id in range(3):
        for col_id in range(3):
            if row_id == col_id:
                entries.append(scales[row_id])
            else:
                entries.append(mixing[3 * row_id + col_id] * jnp.minimum(scales[row_id], scales[col_id]))
    return jnp.stack(entries).astype(jnp.float32)


def draw_mobility(key, part):
    key = jax.random.fold_in(key, 9)
    key_diag, key_mixing = jax.random.split(key)
    cells = (N_GX * 2 * CX, NY * NZ)
    diag_draw = jax.random.uniform(key_diag, (3,) + cells, jnp.float32)
    diagonal = 0.75 + 0.75 * diag_draw
    mixing = jax.random.uniform(key_mixing, (9,) + cells, jnp.float32, -0.1, 0.1)
    entries = []
    for row_id in range(3):
        for col_id in range(3):
            if row_id == col_id:
                entries.append(diagonal[row_id])
            else:
                entries.append(mixing[3 * row_id + col_id])
    return jnp.stack(entries).astype(jnp.float32)


def draw_trans(key, part):
    key = jax.random.fold_in(key, 11)
    cells = (N_GX * 2 * CX, NY * NZ)
    spread_draw = jax.random.uniform(key, (3,) + cells, jnp.float32)
    along = 0.5 * jnp.exp(jnp.log(2.0) * spread_draw[0])
    lateral = 0.02 * jnp.exp(jnp.log(5.0) * spread_draw[1:])
    return jnp.concatenate([along[None], lateral], axis=0).astype(jnp.float32)


def block_scale(own_key, extent, shards, low, largest):
    def one(dim, parts):
        heights = jax.random.uniform(jax.random.fold_in(jax.random.fold_in(own_key, 6), dim), (parts,), jnp.float32, low / len(shards), largest / len(shards))
        return jnp.repeat(jnp.exp(heights), extent[dim] // parts).reshape((-1,) + (1,) * (len(extent) - dim - 1))

    gain = one(*shards[0])
    for cut in shards[1:]:
        gain = gain * one(*cut)
    return gain


def normal_values(stream_key, dims, scale, limit, cuts=(), kind=jnp.bfloat16):
    values = jax.random.normal(stream_key, dims, jnp.float32) * scale
    if len(cuts) > 0:
        values = block_scale(stream_key, dims, cuts, -0.22, 0.18) * values
    return jnp.clip(values, min=-limit, max=limit).astype(kind)


def setup_inputs(seed: int = 0, part: int = 0) -> dict:
    keys = jax.random.split(jax.random.key(seed), 7)
    part_keys = jax.random.split(jax.random.fold_in(keys[6], part), 7)
    return {
        "counts": draw_counts(jax.random.fold_in(jax.random.fold_in(keys[6], part), 71), part),
        "resid": normal_values(part_keys[1], (3, N_GX * CAP, NY * NZ), 1.0, 6.0, ((1, 16),), jnp.float32),
        "accum": draw_accum(jax.random.fold_in(jax.random.fold_in(keys[6], part), 71), part),
        "mobility": draw_mobility(jax.random.fold_in(jax.random.fold_in(keys[6], part), 71), part),
        "trans": draw_trans(jax.random.fold_in(jax.random.fold_in(keys[6], part), 71), part),
        "decouple": jnp.clip(0.3 + 0.7 * jax.random.uniform(part_keys[5], (2, N_GX * CAP, NY * NZ), jnp.float32) ** block_scale(part_keys[5], (2, N_GX * CAP, NY * NZ), ((1, 16),), -0.2, 0.2), 0.3, 1.0),
    }


CHEB_LOW = 0.1
CHEB_HIGH = 2.0


def plane_next(values):
    return jnp.concatenate([values[..., 1:, :], jnp.zeros_like(values[..., :1, :])], axis=-2)


def plane_prev(values):
    return jnp.concatenate([jnp.zeros_like(values[..., :1, :]), values[..., :-1, :]], axis=-2)


def lane_next(values, stride):
    return jnp.concatenate([values[..., stride:], jnp.zeros_like(values[..., :stride])], axis=-1)


def lane_prev(values, stride):
    return jnp.concatenate([jnp.zeros_like(values[..., :stride]), values[..., :-stride]], axis=-1)


def block_mul(blocks, vector):
    return jnp.stack([blocks[3 * row_id] * vector[0] + blocks[3 * row_id + 1] * vector[1] + blocks[3 * row_id + 2] * vector[2] for row_id in range(3)])


def face_sum(trans_plane, trans_row, trans_lane):
    return trans_plane + plane_prev(trans_plane) + trans_row + lane_prev(trans_row, NZ) + trans_lane + lane_prev(trans_lane, 1)


def fine_apply(vector, accum, mobility, trans_plane, trans_row, trans_lane):
    carried = block_mul(mobility, vector)
    across = trans_plane * plane_next(carried) + plane_prev(trans_plane * carried)
    across = across + trans_row * lane_next(carried, NZ) + lane_prev(trans_row * carried, NZ)
    across = across + trans_lane * lane_next(carried, 1) + lane_prev(trans_lane * carried, 1)
    return block_mul(accum, vector) + face_sum(trans_plane, trans_row, trans_lane) * carried - across


def block_inverse(accum, mobility, trans_plane, trans_row, trans_lane, keep_mask):
    totals = face_sum(trans_plane, trans_row, trans_lane)
    entries = [accum[entry_id] + totals * mobility[entry_id] for entry_id in range(9)]
    cofactor = [entries[4] * entries[8] - entries[5] * entries[7], entries[2] * entries[7] - entries[1] * entries[8], entries[1] * entries[5] - entries[2] * entries[4],
                entries[5] * entries[6] - entries[3] * entries[8], entries[0] * entries[8] - entries[2] * entries[6], entries[2] * entries[3] - entries[0] * entries[5],
                entries[3] * entries[7] - entries[4] * entries[6], entries[1] * entries[6] - entries[0] * entries[7], entries[0] * entries[4] - entries[1] * entries[3]]
    determinant = entries[0] * cofactor[0] + entries[1] * cofactor[3] + entries[2] * cofactor[6]
    determinant = jnp.where(keep_mask, determinant, 1.0)
    return jnp.stack([value / determinant for value in cofactor])


def pressure_coefficients(mobile, storage, trans_plane, trans_row, trans_lane):
    coef_plane = trans_plane * (mobile + plane_next(mobile)) * 0.5
    coef_row = trans_row * (mobile + lane_next(mobile, NZ)) * 0.5
    coef_lane = trans_lane * (mobile + lane_next(mobile, 1)) * 0.5
    pivots = storage + coef_plane + plane_prev(coef_plane) + coef_row + lane_prev(coef_row, NZ) + coef_lane + lane_prev(coef_lane, 1)
    return (coef_plane, coef_row, coef_lane, pivots)


def pressure_apply(vector, coeffs):
    coef_plane, coef_row, coef_lane, pivots = coeffs
    across = coef_plane * plane_next(vector) + plane_prev(coef_plane * vector)
    across = across + coef_row * lane_next(vector, NZ) + lane_prev(coef_row * vector, NZ)
    across = across + coef_lane * lane_next(vector, 1) + lane_prev(coef_lane * vector, 1)
    return pivots * vector - across


def chebyshev(source, coeffs):
    inverse = 1.0 / coeffs[3]
    middle = 0.5 * (CHEB_HIGH + CHEB_LOW)
    radius = 0.5 * (CHEB_HIGH - CHEB_LOW)
    aspect = middle / radius
    factor = 1.0 / aspect
    solution = jnp.zeros_like(source)
    remain = source
    direction = inverse * remain / middle
    for iteration in range(CHEB):
        applied = pressure_apply(direction, coeffs)
        solution = solution + direction
        remain = remain - applied
        factor_next = 1.0 / (2.0 * aspect - factor)
        direction = factor_next * factor * direction + (2.0 * factor_next / radius) * inverse * remain
        factor = factor_next
    return solution


def reference(counts, resid, accum, mobility, trans, decouple):
    lane_ids = jnp.arange(NY * NZ)
    keep_rows = ((lane_ids // NZ) < NY - 1).astype(jnp.float32)
    keep_lanes = ((lane_ids % NZ) < NZ - 1).astype(jnp.float32)
    keep_planes = (jnp.arange(NX) < NX - 1).astype(jnp.float32)
    starts = (jnp.cumsum(counts) - counts).astype(jnp.int32)
    slot_ids = jnp.arange(N_GX * CAP).astype(jnp.int32)
    owners = slot_ids // CAP
    within = slot_ids % CAP
    planes = jnp.where(within < counts[owners], starts[owners] + within, NX).astype(jnp.int32)

    def spread(values):
        return jnp.zeros((values.shape[0], NX, NY * NZ), jnp.float32).at[:, planes, :].set(values, mode="drop")

    residual_grid = spread(resid)
    accum_grid = spread(accum)
    mobility_grid = spread(mobility)
    trans_grid = spread(trans)
    decouple_grid = spread(decouple)
    trans_plane = trans_grid[0] * keep_planes[:, None]
    trans_row = trans_grid[1] * keep_rows[None, :]
    trans_lane = trans_grid[2] * keep_lanes[None, :]
    weight_one = decouple_grid[0]
    weight_two = decouple_grid[1]
    source = residual_grid[0] + weight_one * residual_grid[1] + weight_two * residual_grid[2]
    mobile = mobility_grid[0] + weight_one * mobility_grid[3] + weight_two * mobility_grid[6]
    storage = accum_grid[0] + weight_one * accum_grid[3] + weight_two * accum_grid[6]
    coeffs = pressure_coefficients(mobile, storage, trans_plane, trans_row, trans_lane)
    pressure = chebyshev(source, coeffs)
    blank = jnp.zeros_like(pressure)
    lifted = jnp.stack([pressure, blank, blank])
    updated = residual_grid - fine_apply(lifted, accum_grid, mobility_grid, trans_plane, trans_row, trans_lane)
    stacked = jnp.concatenate([accum_grid, mobility_grid, trans_plane[None], trans_row[None], trans_lane[None], updated, lifted], axis=0)
    padded = jnp.pad(stacked, ((0, 0), (3, CAP + 3), (0, 0)))

    def one_part(owner_id):
        first_plane = starts[owner_id]
        plane_count = counts[owner_id]
        window = lax.dynamic_slice_in_dim(padded, first_plane, CAP + 6, axis=1)
        ext_ids = jnp.arange(CAP + 6).astype(jnp.int32)
        global_ids = first_plane - 3 + ext_ids
        inside = (ext_ids >= 1) & (ext_ids < plane_count + 5) & (global_ids >= 0) & (global_ids < NX)
        owned = (ext_ids >= 3) & (ext_ids < plane_count + 3)
        sub_accum = window[0:9]
        sub_mobility = window[9:18]
        sub_plane = window[18]
        sub_row = window[19]
        sub_lane = window[20]
        target = jnp.where(inside[:, None], window[21:24], 0.0)
        sub_lifted = window[24:27]
        inverse = block_inverse(sub_accum, sub_mobility, sub_plane, sub_row, sub_lane, inside[:, None])
        local = jnp.zeros_like(target)
        for sweep_id in range(SWEEPS):
            defect = target - fine_apply(local, sub_accum, sub_mobility, sub_plane, sub_row, sub_lane)
            local = jnp.where(inside[:, None], local + block_mul(inverse, defect), 0.0)
        return jnp.where(owned[:, None], sub_lifted + local, 0.0)[:, 3:3 + CAP]

    results = lax.map(one_part, jnp.arange(N_GX).astype(jnp.int32))
    return jnp.transpose(results, (1, 0, 2, 3)).reshape(3, N_GX * CAP, NY * NZ)
```

```python
import functools

import jax
import jax.numpy as jnp
from jax import lax
from jax.experimental import pallas as pl
from jax.experimental.pallas import tpu as pltpu
from jax.sharding import PartitionSpec as P

CX = 8
NZ = 32
CHEB = 6
SWEEPS = 6
CAP = 16
CHEB_LOW = 0.1
CHEB_HIGH = 2.0

LEAD = 7
OWN = LEAD + CAP
PW = 30
FW = 18
SW = 16
HALO = 11


def y_next(x, lane):
    r = pltpu.roll(x, 96, x.ndim - 1)
    return jnp.where(lane < 96, r, pltpu.roll(r, 7, x.ndim - 2))


def y_prev(x, lane):
    r = pltpu.roll(x, 32, x.ndim - 1)
    return jnp.where(lane >= 32, r, pltpu.roll(r, 1, x.ndim - 2))


def z_next(x):
    return pltpu.roll(x, 127, x.ndim - 1)


def z_prev(x):
    return pltpu.roll(x, 1, x.ndim - 1)


def kernel(
    n,
    counts,
    resid,
    accum,
    mobility,
    trans,
    decouple,
    out,
    own,
    pown,
    below1,
    above1,
    below2,
    above2,
    fup,
    fbelow,
    fabove,
    pw,
    coef,
    direction,
    remain,
    total,
    fine,
    blocks,
    carried,
    target,
    result,
    send_sem,
    recv_sem,
):
    me = lax.axis_index("gx")
    grid = CX * n
    barrier = pltpu.get_barrier_semaphore()
    here = {}
    for step in (-2, -1, 1, 2):
        here[step] = (me + step >= 0) & (me + step < n)

        @pl.when(here[step])
        def _():
            pl.semaphore_signal(
                barrier, inc=1, device_id={"gx": me + step}, device_id_type=pl.DeviceIdType.MESH
            )

    start = jnp.int32(0)
    for part in range(n):
        start = start + jnp.where(part < me, counts[part], 0)
    count = counts[me]
    end = start + count
    base = CX * me
    drift = jnp.clip(start - base, -2, 2)
    drift_end = jnp.clip(end - base - CX, -2, 2)

    shape = (1, 8, 128)
    lane = lax.broadcasted_iota(jnp.int32, shape, 2)
    row = lax.broadcasted_iota(jnp.int32, shape, 1)
    keep_row = jnp.where((row < 7) | (lane < 96), 1.0, 0.0)
    keep_lane = jnp.where(lane % NZ < NZ - 1, 1.0, 0.0)

    def planes(first, length):
        return first + lax.broadcasted_iota(jnp.int32, (length, 8, 128), 0)

    blank = jnp.zeros((LEAD, 8, 128), jnp.float32)
    order = [(mobility, i) for i in range(9)] + [(accum, i) for i in range(9)]
    order += [(resid, i) for i in range(3)] + [(trans, i) for i in range(3)]
    order += [(decouple, i) for i in range(2)]
    spans = [(mobility, 0, 9), (accum, 9, 9), (resid, 18, 3), (trans, 21, 3), (decouple, 24, 2)]
    for ref, first, length in spans:

        def place(i, _, ref=ref, first=first):
            own[first + i, :LEAD] = blank
            own[first + i, LEAD:] = ref[i].reshape(CAP, 8, 128)
            return 0

        lax.fori_loop(0, length, place, 0)

    at = 5 - drift
    spot = planes(base - 2, 12)
    mine = (spot >= start) & (spot < end)

    def field(i):
        return own[i, pl.ds(at, 12)]

    one, two = field(24), field(25)
    pown[0] = jnp.where(mine, field(18) + one * field(19) + two * field(20), 0.0)
    pown[1] = jnp.where(mine, field(0) + one * field(3) + two * field(6), 0.0)
    pown[2] = jnp.where(mine, field(9) + one * field(12) + two * field(15), 0.0)
    pown[3] = jnp.where(mine & (spot < grid - 1), field(21), 0.0)
    pown[4] = jnp.where(mine, field(22) * keep_row, 0.0)
    pown[5] = jnp.where(mine, field(23) * keep_lane, 0.0)

    for i in range(21):
        fup[i] = own[i, pl.ds(LEAD + jnp.clip(count, 4, 12) - 3, 3)]

    for step, ref in ((-1, below1), (1, above1), (-2, below2), (2, above2)):

        @pl.when(jnp.logical_not(here[step]))
        def _():
            ref[...] = jnp.zeros_like(ref)

    known = jnp.int32(0)
    for step in here:
        known = known + here[step].astype(jnp.int32)
    pl.semaphore_wait(barrier, known)

    def send(src, dst, step, slot):
        return pltpu.make_async_remote_copy(
            src_ref=src,
            dst_ref=dst,
            send_sem=send_sem.at[slot],
            recv_sem=recv_sem.at[slot],
            device_id={"gx": me + step},
            device_id_type=pl.DeviceIdType.MESH,
        )

    copies = [
        (1, send(pown, below1, 1, 0)),
        (-1, send(pown, above1, -1, 1)),
        (2, send(pown.at[:, 7:12], below2, 2, 2)),
        (-2, send(pown.at[:, 0:5], above2, -2, 3)),
        (1, send(fup, fbelow.at[:, 4:7], 1, 4)),
        (-1, send(own.at[0:21, LEAD : LEAD + 3], fabove.at[:, 4:7], -1, 5)),
    ]
    for step, copy in copies:

        @pl.when(here[step])
        def _():
            copy.start()

    for step, copy in copies[:4]:

        @pl.when(here[-step])
        def _():
            copy.wait_recv()

    for i in range(6):
        pw[i, 0:1] = below2[i, 0:1]
        pw[i, 1:5] = below2[i, 1:5] + below1[i, 0:4]
        pw[i, 5:9] = below1[i, 4:8]
        pw[i, 9:13] = below1[i, 8:12] + pown[i, 0:4]
        pw[i, 13:17] = pown[i, 4:8]
        pw[i, 17:21] = pown[i, 8:12] + above1[i, 0:4]
        pw[i, 21:25] = above1[i, 4:8]
        pw[i, 25:29] = above1[i, 8:12] + above2[i, 0:4]
        pw[i, 29:30] = above2[i, 4:5]
    zero = jnp.zeros((1, 8, 128), jnp.float32)
    for i in range(2):
        direction[i, 0:1] = zero
        direction[i, PW - 1 : PW] = zero

    middle = 0.5 * (CHEB_HIGH + CHEB_LOW)
    radius = 0.5 * (CHEB_HIGH - CHEB_LOW)
    aspect = middle / radius
    PC = 4

    def prepare(j, _):
        k = 1 + j * PC
        lam = pw[1, pl.ds(k, PC)]
        lam_up = pw[1, pl.ds(k + 1, PC)]
        lam_down = pw[1, pl.ds(k - 1, PC)]
        tx_down = pw[3, pl.ds(k - 1, PC)]
        cx = pw[3, pl.ds(k, PC)] * (lam + lam_up) * 0.5
        cx_down = tx_down * (lam_down + lam) * 0.5
        cy = pw[4, pl.ds(k, PC)] * (lam + y_next(lam, lane)) * 0.5
        cz = pw[5, pl.ds(k, PC)] * (lam + z_next(lam)) * 0.5
        cy_down = y_prev(cy, lane)
        cz_down = z_prev(cz)
        pivot = pw[2, pl.ds(k, PC)] + cx + cx_down + cy + cy_down + cz + cz_down
        where = planes(base - 11 + k, PC)
        inverse = 1.0 / jnp.where((where >= 0) & (where < grid), pivot, 1.0)
        for i, value in enumerate((cx, cx_down, cy, cy_down, cz, cz_down)):
            coef[i, pl.ds(k, PC)] = value * inverse
        scaled = pw[0, pl.ds(k, PC)] * inverse
        remain[pl.ds(k, PC)] = scaled
        first = scaled / middle
        direction[0, pl.ds(k, PC)] = first
        total[pl.ds(k, PC)] = first
        return 0

    lax.fori_loop(0, (PW - 2) // PC, prepare, 0)

    factor = 1.0 / aspect
    for iteration in range(CHEB - 1):
        now, later = iteration % 2, (iteration + 1) % 2
        factor_next = 1.0 / (2.0 * aspect - factor)

        def advance(j, _, now=now, later=later, factor=factor, factor_next=factor_next):
            k = 1 + j * PC
            d = direction[now, pl.ds(k, PC)]
            across = coef[0, pl.ds(k, PC)] * direction[now, pl.ds(k + 1, PC)]
            across = across + coef[1, pl.ds(k, PC)] * direction[now, pl.ds(k - 1, PC)]
            across = across + coef[2, pl.ds(k, PC)] * y_next(d, lane)
            across = across + coef[3, pl.ds(k, PC)] * y_prev(d, lane)
            across = across + coef[4, pl.ds(k, PC)] * z_next(d)
            across = across + coef[5, pl.ds(k, PC)] * z_prev(d)
            e = remain[pl.ds(k, PC)] - d + across
            remain[pl.ds(k, PC)] = e
            d = (factor_next * factor) * d + (2.0 * factor_next / radius) * e
            direction[later, pl.ds(k, PC)] = d
            total[pl.ds(k, PC)] = total[pl.ds(k, PC)] + d
            return 0

        lax.fori_loop(0, (PW - 2) // PC, advance, 0)
        factor = factor_next

    for step, copy in copies[4:]:

        @pl.when(here[-step])
        def _():
            copy.wait_recv()

    at_own = 2 - drift
    at_below = 2 - drift
    at_above = 2 - drift_end
    spot_low = planes(base - 5, 7)
    spot_mid = planes(base + 2, 4)
    spot_high = planes(base + 6, 7)

    def owned(spot):
        return (spot >= start) & (spot < end)

    low_mine, mid_mine, high_mine = owned(spot_low), owned(spot_mid), owned(spot_high)
    low_near = (spot_low >= start - 3) & (spot_low < start) & (spot_low >= 0)
    high_near = (spot_high >= end) & (spot_high < end + 3) & (spot_high < grid)

    def assemble(i, _):
        low = jnp.where(low_near, fbelow[i, pl.ds(at_below, 7)], 0.0)
        high = jnp.where(high_near, fabove[i, pl.ds(at_above, 7)], 0.0)
        fine[i, 0:7] = jnp.where(low_mine, own[i, pl.ds(at_own, 7)], low)
        fine[i, 7:11] = jnp.where(mid_mine, own[i, pl.ds(at_own + 7, 4)], 0.0)
        fine[i, 11:18] = jnp.where(high_mine, own[i, pl.ds(at_own + 11, 7)], high)
        return 0

    lax.fori_loop(0, 21, assemble, 0)

    for i in range(3):
        for slot in range(2):
            carried[slot, i, 0:1] = zero
            carried[slot, i, FW - 1 : FW] = zero
        carried[1, i] = fine[3 * i] * total[6 : 6 + FW]

    def across_of(slot, k, size):
        tx = pw[3, pl.ds(k + 6, size)]
        tx_down = pw[3, pl.ds(k + 5, size)]
        ty = pw[4, pl.ds(k + 6, size)]
        tz = pw[5, pl.ds(k + 6, size)]
        ty_down = y_prev(ty, lane)
        tz_down = z_prev(tz)
        sums = []
        for i in range(3):
            u = carried[slot, i, pl.ds(k, size)]
            value = tx * carried[slot, i, pl.ds(k + 1, size)]
            value = value + tx_down * carried[slot, i, pl.ds(k - 1, size)]
            value = value + ty * y_next(u, lane) + ty_down * y_prev(u, lane)
            value = value + tz * z_next(u) + tz_down * z_prev(u)
            sums.append(value)
        return sums, tx + tx_down + ty + ty_down + tz + tz_down

    def times(first, k, size, vector):
        return [
            blocks[first + 3 * i, pl.ds(k, size)] * vector[0]
            + blocks[first + 3 * i + 1, pl.ds(k, size)] * vector[1]
            + blocks[first + 3 * i + 2, pl.ds(k, size)] * vector[2]
            for i in range(3)
        ]

    SC = 2

    def invert(j, _):
        k = 1 + j * SC
        sums, faces = across_of(1, k, SC)
        m = [fine[i, pl.ds(k, SC)] for i in range(9)]
        b = [fine[9 + i, pl.ds(k, SC)] + faces * m[i] for i in range(9)]
        p = total[pl.ds(k + 6, SC)]
        where = planes(base - 5 + k, SC)
        inside = (where >= start - 2) & (where < end + 2) & (where >= 0) & (where < grid)
        goal = [
            jnp.where(inside, fine[18 + i, pl.ds(k, SC)] - b[3 * i] * p + sums[i], 0.0)
            for i in range(3)
        ]
        for i in range(3):
            target[i, pl.ds(k, SC)] = goal[i]
        cofactor = [
            b[4] * b[8] - b[5] * b[7],
            b[2] * b[7] - b[1] * b[8],
            b[1] * b[5] - b[2] * b[4],
            b[5] * b[6] - b[3] * b[8],
            b[0] * b[8] - b[2] * b[6],
            b[2] * b[3] - b[0] * b[5],
            b[3] * b[7] - b[4] * b[6],
            b[1] * b[6] - b[0] * b[7],
            b[0] * b[4] - b[1] * b[3],
        ]
        det = b[0] * cofactor[0] + b[1] * cofactor[3] + b[2] * cofactor[6]
        scale = 1.0 / jnp.where(inside, det, 1.0)
        inv = [jnp.where(inside, value * scale, 0.0) for value in cofactor]
        for i in range(3):
            value = 0.0
            for c in range(3):
                blocks[3 * i + c, pl.ds(k, SC)] = inv[3 * i + c]
                g = m[3 * i] * inv[c] + m[3 * i + 1] * inv[3 + c] + m[3 * i + 2] * inv[6 + c]
                blocks[9 + 3 * i + c, pl.ds(k, SC)] = g
                value = value + g * goal[c]
            carried[0, i, pl.ds(k, SC)] = value
        return 0

    lax.fori_loop(0, SW // SC, invert, 0)
    for i in range(3):
        carried[1, i, 0:1] = zero
        carried[1, i, FW - 1 : FW] = zero

    for sweep in range(SWEEPS - 1):
        now, later = sweep % 2, (sweep + 1) % 2

        def relax(j, _, now=now, later=later, last=sweep == SWEEPS - 2):
            k = 1 + j * SC
            sums, _ = across_of(now, k, SC)
            vector = [target[i, pl.ds(k, SC)] + sums[i] for i in range(3)]
            new = times(0 if last else 9, k, SC, vector)
            if last:
                new[0] = new[0] + total[pl.ds(k + 6, SC)]
            for i in range(3):
                if last:
                    result[i, pl.ds(k, SC)] = new[i]
                else:
                    carried[later, i, pl.ds(k, SC)] = new[i]
            return 0

        lax.fori_loop(0, SW // SC, relax, 0)

    slot_ids = planes(0, CAP)
    for i in range(3):
        value = result[i, pl.ds(drift + 5, CAP)]
        out[i] = jnp.where(slot_ids < count, value, 0.0)

    for step, copy in copies:

        @pl.when(here[step])
        def _():
            copy.wait_send()


def on_device(counts, resid, accum, mobility, trans, decouple):
    n = lax.axis_size("gx")
    f32 = jnp.float32

    def vmem(*dims):
        return pltpu.VMEM(dims + (8, 128), f32)

    value = pl.pallas_call(
        functools.partial(kernel, n),
        out_shape=jax.ShapeDtypeStruct((3, CAP, 8, 128), f32),
        in_specs=[pl.BlockSpec(memory_space=pltpu.SMEM)]
        + [pl.BlockSpec(memory_space=pltpu.VMEM)] * 5,
        out_specs=pl.BlockSpec(memory_space=pltpu.VMEM),
        scratch_shapes=[
            vmem(26, OWN),
            vmem(6, 12),
            vmem(6, 12),
            vmem(6, 12),
            vmem(6, 5),
            vmem(6, 5),
            vmem(21, 3),
            vmem(21, HALO),
            vmem(21, HALO),
            vmem(6, PW),
            vmem(6, PW),
            vmem(2, PW),
            vmem(PW),
            vmem(PW),
            vmem(21, FW),
            vmem(18, FW),
            vmem(2, 3, FW),
            vmem(3, FW),
            vmem(3, 24),
            pltpu.SemaphoreType.DMA((6,)),
            pltpu.SemaphoreType.DMA((6,)),
        ],
        compiler_params=pltpu.CompilerParams(
            collective_id=0, has_side_effects=True, vmem_limit_bytes=40 * 1024 * 1024
        ),
    )(counts, resid, accum, mobility, trans, decouple)
    return value.reshape(3, CAP, 1024)


def solution(mesh):
    spec = P(None, ("groups", "gx"), None)
    return jax.shard_map(
        on_device,
        mesh=mesh,
        in_specs=(P("groups"),) + (spec,) * 5,
        out_specs=spec,
        check_vma=False,
    )
```

```python
import functools

import jax
import jax.numpy as jnp
from jax import lax
from jax.experimental import pallas as pl
from jax.experimental.pallas import tpu as pltpu
from jax.sharding import PartitionSpec as P

CX = 8
NZ = 32
CHEB = 6
SWEEPS = 6
CAP = 16
CHEB_LOW = 0.1
CHEB_HIGH = 2.0

LEAD = 7
OWN = LEAD + CAP
PW = 30
FW = 18
SW = 16
HALO = 11


def y_next(x, lane):
    r = pltpu.roll(x, 96, x.ndim - 1)
    return jnp.where(lane < 96, r, pltpu.roll(r, 7, x.ndim - 2))


def y_prev(x, lane):
    r = pltpu.roll(x, 32, x.ndim - 1)
    return jnp.where(lane >= 32, r, pltpu.roll(r, 1, x.ndim - 2))


def z_next(x):
    return pltpu.roll(x, 127, x.ndim - 1)


def z_prev(x):
    return pltpu.roll(x, 1, x.ndim - 1)


def kernel(
    n,
    counts_hbm,
    resid_hbm,
    accum_hbm,
    mobility_hbm,
    trans_hbm,
    decouple_hbm,
    out,
    counts,
    resid,
    accum,
    mobility,
    trans,
    decouple,
    own,
    pown,
    below1,
    above1,
    below2,
    above2,
    fup,
    fbelow,
    fabove,
    pw,
    coef,
    direction,
    remain,
    total,
    fine,
    blocks,
    carried,
    target,
    result,
    send_sem,
    recv_sem,
    load_sem,
):
    me = lax.axis_index("gx")
    pairs = [
        (counts_hbm, counts),
        (mobility_hbm, mobility),
        (accum_hbm, accum),
        (resid_hbm, resid),
        (trans_hbm, trans),
        (decouple_hbm, decouple),
    ]
    loads = [
        pltpu.make_async_copy(src, dst, load_sem.at[i]) for i, (src, dst) in enumerate(pairs)
    ]
    for load in loads:
        load.start()
    grid = CX * n
    barrier = pltpu.get_barrier_semaphore()
    here = {}
    for step in (-2, -1, 1, 2):
        here[step] = (me + step >= 0) & (me + step < n)

        @pl.when(here[step])
        def _():
            pl.semaphore_signal(
                barrier, inc=1, device_id={"gx": me + step}, device_id_type=pl.DeviceIdType.MESH
            )

    loads[0].wait()
    start = jnp.int32(0)
    for part in range(n):
        start = start + jnp.where(part < me, counts[part], 0)
    count = counts[me]
    end = start + count
    base = CX * me
    drift = jnp.clip(start - base, -2, 2)
    drift_end = jnp.clip(end - base - CX, -2, 2)

    shape = (1, 8, 128)
    lane = lax.broadcasted_iota(jnp.int32, shape, 2)
    row = lax.broadcasted_iota(jnp.int32, shape, 1)
    keep_row = jnp.where((row < 7) | (lane < 96), 1.0, 0.0)
    keep_lane = jnp.where(lane % NZ < NZ - 1, 1.0, 0.0)

    def planes(first, length):
        return first + lax.broadcasted_iota(jnp.int32, (length, 8, 128), 0)

    blank = jnp.zeros((LEAD, 8, 128), jnp.float32)
    columns = (0, 3, 6, 1, 2, 4, 5, 7, 8)
    place_of = {c: i for i, c in enumerate(columns)}

    def place(i, ref, at):
        own[i, :LEAD] = blank
        own[i, LEAD:] = ref[at].reshape(CAP, 8, 128)

    for load in loads[1:]:
        load.wait()
    for i in range(3):
        place(i, mobility, 3 * i)
        place(9 + 3 * i, accum, 3 * i)
        place(18 + i, resid, i)
        place(21 + i, trans, i)
    for i in range(2):
        place(24 + i, decouple, i)

    at = 5 - drift
    spot = planes(base - 2, 12)
    mine = (spot >= start) & (spot < end)

    def field(i):
        return own[i, pl.ds(at, 12)]

    one, two = field(24), field(25)
    pown[0] = jnp.where(mine, field(18) + one * field(19) + two * field(20), 0.0)
    pown[1] = jnp.where(mine, field(0) + one * field(1) + two * field(2), 0.0)
    pown[2] = jnp.where(mine, field(9) + one * field(12) + two * field(15), 0.0)
    pown[3] = jnp.where(mine & (spot < grid - 1), field(21), 0.0)
    pown[4] = jnp.where(mine, field(22) * keep_row, 0.0)
    pown[5] = jnp.where(mine, field(23) * keep_lane, 0.0)

    for step, ref in ((-1, below1), (1, above1), (-2, below2), (2, above2)):

        @pl.when(jnp.logical_not(here[step]))
        def _():
            ref[...] = jnp.zeros_like(ref)

    known = jnp.int32(0)
    for step in here:
        known = known + here[step].astype(jnp.int32)
    pl.semaphore_wait(barrier, known)

    def send(src, dst, step, slot):
        return pltpu.make_async_remote_copy(
            src_ref=src,
            dst_ref=dst,
            send_sem=send_sem.at[slot],
            recv_sem=recv_sem.at[slot],
            device_id={"gx": me + step},
            device_id_type=pl.DeviceIdType.MESH,
        )

    copies = [
        (1, send(pown, below1, 1, 0)),
        (-1, send(pown, above1, -1, 1)),
        (2, send(pown.at[:, 7:12], below2, 2, 2)),
        (-2, send(pown.at[:, 0:5], above2, -2, 3)),
        (1, send(fup.at[0:3], fbelow.at[0:3, 4:7], 1, 4)),
        (1, send(fup.at[3:21, 1:3], fbelow.at[3:21, 5:7], 1, 5)),
        (-1, send(own.at[0:3, LEAD : LEAD + 3], fabove.at[0:3, 4:7], -1, 6)),
        (-1, send(own.at[3:21, LEAD : LEAD + 2], fabove.at[3:21, 4:6], -1, 7)),
    ]

    def start_all(some):
        for step, copy in some:

            @pl.when(here[step])
            def _():
                copy.start()

    start_all(copies[:4])
    for i in range(3):
        for c in (1, 2):
            place(place_of[3 * i + c], mobility, 3 * i + c)
            place(9 + 3 * i + c, accum, 3 * i + c)
    for i in range(21):
        fup[i] = own[i, pl.ds(LEAD + jnp.clip(count, 4, 12) - 3, 3)]
    start_all(copies[4:])

    for step, copy in copies[:4]:

        @pl.when(here[-step])
        def _():
            copy.wait_recv()

    for i in range(6):
        pw[i, 0:1] = below2[i, 0:1]
        pw[i, 1:5] = below2[i, 1:5] + below1[i, 0:4]
        pw[i, 5:9] = below1[i, 4:8]
        pw[i, 9:13] = below1[i, 8:12] + pown[i, 0:4]
        pw[i, 13:17] = pown[i, 4:8]
        pw[i, 17:21] = pown[i, 8:12] + above1[i, 0:4]
        pw[i, 21:25] = above1[i, 4:8]
        pw[i, 25:29] = above1[i, 8:12] + above2[i, 0:4]
        pw[i, 29:30] = above2[i, 4:5]
    zero = jnp.zeros((1, 8, 128), jnp.float32)
    for i in range(2):
        direction[i, 0:1] = zero
        direction[i, PW - 1 : PW] = zero

    middle = 0.5 * (CHEB_HIGH + CHEB_LOW)
    radius = 0.5 * (CHEB_HIGH - CHEB_LOW)
    aspect = middle / radius
    PC = 4

    def prepare(j, _):
        k = 1 + j * PC
        lam = pw[1, pl.ds(k, PC)]
        lam_up = pw[1, pl.ds(k + 1, PC)]
        lam_down = pw[1, pl.ds(k - 1, PC)]
        tx_down = pw[3, pl.ds(k - 1, PC)]
        cx = pw[3, pl.ds(k, PC)] * (lam + lam_up) * 0.5
        cx_down = tx_down * (lam_down + lam) * 0.5
        cy = pw[4, pl.ds(k, PC)] * (lam + y_next(lam, lane)) * 0.5
        cz = pw[5, pl.ds(k, PC)] * (lam + z_next(lam)) * 0.5
        cy_down = y_prev(cy, lane)
        cz_down = z_prev(cz)
        pivot = pw[2, pl.ds(k, PC)] + cx + cx_down + cy + cy_down + cz + cz_down
        where = planes(base - 11 + k, PC)
        inverse = 1.0 / jnp.where((where >= 0) & (where < grid), pivot, 1.0)
        for i, value in enumerate((cx, cx_down, cy, cy_down, cz, cz_down)):
            coef[i, pl.ds(k, PC)] = value * inverse
        scaled = pw[0, pl.ds(k, PC)] * inverse
        remain[pl.ds(k, PC)] = scaled
        first = scaled / middle
        direction[0, pl.ds(k, PC)] = first
        total[pl.ds(k, PC)] = first
        return 0

    lax.fori_loop(0, (PW - 2) // PC, prepare, 0)

    factor = 1.0 / aspect
    for iteration in range(CHEB - 1):
        now, later = iteration % 2, (iteration + 1) % 2
        factor_next = 1.0 / (2.0 * aspect - factor)

        def advance(j, _, now=now, later=later, factor=factor, factor_next=factor_next):
            k = 1 + j * PC
            d = direction[now, pl.ds(k, PC)]
            across = coef[0, pl.ds(k, PC)] * direction[now, pl.ds(k + 1, PC)]
            across = across + coef[1, pl.ds(k, PC)] * direction[now, pl.ds(k - 1, PC)]
            across = across + coef[2, pl.ds(k, PC)] * y_next(d, lane)
            across = across + coef[3, pl.ds(k, PC)] * y_prev(d, lane)
            across = across + coef[4, pl.ds(k, PC)] * z_next(d)
            across = across + coef[5, pl.ds(k, PC)] * z_prev(d)
            e = remain[pl.ds(k, PC)] - d + across
            remain[pl.ds(k, PC)] = e
            d = (factor_next * factor) * d + (2.0 * factor_next / radius) * e
            direction[later, pl.ds(k, PC)] = d
            total[pl.ds(k, PC)] = total[pl.ds(k, PC)] + d
            return 0

        lax.fori_loop(0, (PW - 2) // PC, advance, 0)
        factor = factor_next

    for step, copy in copies[4:]:

        @pl.when(here[-step])
        def _():
            copy.wait_recv()

    at_own = 2 - drift
    at_below = 2 - drift
    at_above = 2 - drift_end
    spot_low = planes(base - 5, 7)
    spot_mid = planes(base + 2, 4)
    spot_high = planes(base + 6, 7)

    def owned(spot):
        return (spot >= start) & (spot < end)

    low_mine, mid_mine, high_mine = owned(spot_low), owned(spot_mid), owned(spot_high)
    for first, last, width in ((0, 3, 3), (3, 21, 2)):
        low_near = (spot_low >= start - width) & (spot_low < start) & (spot_low >= 0)
        high_near = (spot_high >= end) & (spot_high < end + width) & (spot_high < grid)

        def assemble(i, _, low_near=low_near, high_near=high_near):
            low = jnp.where(low_near, fbelow[i, pl.ds(at_below, 7)], 0.0)
            high = jnp.where(high_near, fabove[i, pl.ds(at_above, 7)], 0.0)
            fine[i, 0:7] = jnp.where(low_mine, own[i, pl.ds(at_own, 7)], low)
            fine[i, 7:11] = jnp.where(mid_mine, own[i, pl.ds(at_own + 7, 4)], 0.0)
            fine[i, 11:18] = jnp.where(high_mine, own[i, pl.ds(at_own + 11, 7)], high)
            return 0

        lax.fori_loop(first, last, assemble, 0)

    for i in range(3):
        for slot in range(2):
            carried[slot, i, 0:1] = zero
            carried[slot, i, FW - 1 : FW] = zero
        carried[1, i] = fine[i] * total[6 : 6 + FW]

    def across_of(slot, k, size):
        tx = pw[3, pl.ds(k + 6, size)]
        tx_down = pw[3, pl.ds(k + 5, size)]
        ty = pw[4, pl.ds(k + 6, size)]
        tz = pw[5, pl.ds(k + 6, size)]
        ty_down = y_prev(ty, lane)
        tz_down = z_prev(tz)
        sums = []
        for i in range(3):
            u = carried[slot, i, pl.ds(k, size)]
            value = tx * carried[slot, i, pl.ds(k + 1, size)]
            value = value + tx_down * carried[slot, i, pl.ds(k - 1, size)]
            value = value + ty * y_next(u, lane) + ty_down * y_prev(u, lane)
            value = value + tz * z_next(u) + tz_down * z_prev(u)
            sums.append(value)
        return sums, tx + tx_down + ty + ty_down + tz + tz_down

    def times(first, k, size, vector):
        return [
            blocks[first + 3 * i, pl.ds(k, size)] * vector[0]
            + blocks[first + 3 * i + 1, pl.ds(k, size)] * vector[1]
            + blocks[first + 3 * i + 2, pl.ds(k, size)] * vector[2]
            for i in range(3)
        ]

    SC = 2

    def invert(j, _):
        k = 1 + j * SC
        sums, faces = across_of(1, k, SC)
        m = [fine[place_of[i], pl.ds(k, SC)] for i in range(9)]
        b = [fine[9 + i, pl.ds(k, SC)] + faces * m[i] for i in range(9)]
        p = total[pl.ds(k + 6, SC)]
        where = planes(base - 5 + k, SC)
        inside = (where >= start - 2) & (where < end + 2) & (where >= 0) & (where < grid)
        goal = [
            jnp.where(inside, fine[18 + i, pl.ds(k, SC)] - b[3 * i] * p + sums[i], 0.0)
            for i in range(3)
        ]
        for i in range(3):
            target[i, pl.ds(k, SC)] = goal[i]
        cofactor = [
            b[4] * b[8] - b[5] * b[7],
            b[2] * b[7] - b[1] * b[8],
            b[1] * b[5] - b[2] * b[4],
            b[5] * b[6] - b[3] * b[8],
            b[0] * b[8] - b[2] * b[6],
            b[2] * b[3] - b[0] * b[5],
            b[3] * b[7] - b[4] * b[6],
            b[1] * b[6] - b[0] * b[7],
            b[0] * b[4] - b[1] * b[3],
        ]
        det = b[0] * cofactor[0] + b[1] * cofactor[3] + b[2] * cofactor[6]
        scale = 1.0 / jnp.where(inside, det, 1.0)
        inv = [jnp.where(inside, value * scale, 0.0) for value in cofactor]
        for i in range(3):
            value = 0.0
            for c in range(3):
                blocks[3 * i + c, pl.ds(k, SC)] = inv[3 * i + c]
                g = m[3 * i] * inv[c] + m[3 * i + 1] * inv[3 + c] + m[3 * i + 2] * inv[6 + c]
                blocks[9 + 3 * i + c, pl.ds(k, SC)] = g
                value = value + g * goal[c]
            carried[0, i, pl.ds(k, SC)] = value
        return 0

    lax.fori_loop(0, SW // SC, invert, 0)
    for i in range(3):
        carried[1, i, 0:1] = zero
        carried[1, i, FW - 1 : FW] = zero

    for sweep in range(SWEEPS - 1):
        now, later = sweep % 2, (sweep + 1) % 2

        def relax(j, _, now=now, later=later, last=sweep == SWEEPS - 2):
            k = 1 + j * SC
            sums, _ = across_of(now, k, SC)
            vector = [target[i, pl.ds(k, SC)] + sums[i] for i in range(3)]
            new = times(0 if last else 9, k, SC, vector)
            if last:
                new[0] = new[0] + total[pl.ds(k + 6, SC)]
            for i in range(3):
                if last:
                    result[i, pl.ds(k, SC)] = new[i]
                else:
                    carried[later, i, pl.ds(k, SC)] = new[i]
            return 0

        lax.fori_loop(0, SW // SC, relax, 0)

    slot_ids = planes(0, CAP)
    for i in range(3):
        value = result[i, pl.ds(drift + 5, CAP)]
        out[i] = jnp.where(slot_ids < count, value, 0.0)

    for step, copy in copies:

        @pl.when(here[step])
        def _():
            copy.wait_send()


def on_device(counts, resid, accum, mobility, trans, decouple):
    n = lax.axis_size("gx")
    f32 = jnp.float32

    def vmem(*dims):
        return pltpu.VMEM(dims + (8, 128), f32)

    value = pl.pallas_call(
        functools.partial(kernel, n),
        out_shape=jax.ShapeDtypeStruct((3, CAP, 8, 128), f32),
        in_specs=[pl.BlockSpec(memory_space=pltpu.HBM)] * 6,
        out_specs=pl.BlockSpec(memory_space=pltpu.VMEM),
        scratch_shapes=[
            pltpu.SMEM((n,), jnp.int32),
            pltpu.VMEM((3, CAP, 1024), f32),
            pltpu.VMEM((9, CAP, 1024), f32),
            pltpu.VMEM((9, CAP, 1024), f32),
            pltpu.VMEM((3, CAP, 1024), f32),
            pltpu.VMEM((2, CAP, 1024), f32),
            vmem(26, OWN),
            vmem(6, 12),
            vmem(6, 12),
            vmem(6, 12),
            vmem(6, 5),
            vmem(6, 5),
            vmem(21, 3),
            vmem(21, HALO),
            vmem(21, HALO),
            vmem(6, PW),
            vmem(6, PW),
            vmem(2, PW),
            vmem(PW),
            vmem(PW),
            vmem(21, FW),
            vmem(18, FW),
            vmem(2, 3, FW),
            vmem(3, FW),
            vmem(3, 24),
            pltpu.SemaphoreType.DMA((8,)),
            pltpu.SemaphoreType.DMA((8,)),
            pltpu.SemaphoreType.DMA((6,)),
        ],
        compiler_params=pltpu.CompilerParams(
            collective_id=0, has_side_effects=True, vmem_limit_bytes=64 * 1024 * 1024
        ),
    )(counts, resid, accum, mobility, trans, decouple)
    return value.reshape(3, CAP, 1024)


def solution(mesh):
    spec = P(None, ("groups", "gx"), None)
    return jax.shard_map(
        on_device,
        mesh=mesh,
        in_specs=(P("groups"),) + (spec,) * 5,
        out_specs=spec,
        check_vma=False,
    )
```

```python
import functools

import jax
import jax.numpy as jnp
from jax import lax
from jax.experimental import pallas as pl
from jax.experimental.pallas import tpu as pltpu
from jax.sharding import PartitionSpec as P

CX = 8
NZ = 32
CHEB = 6
SWEEPS = 6
CAP = 16
CHEB_LOW = 0.1
CHEB_HIGH = 2.0

LEAD = 7
OWN = LEAD + CAP
PW = 30
FW = 18
SW = 16
HALO = 11


def y_next(x, lane):
    r = pltpu.roll(x, 96, x.ndim - 1)
    return jnp.where(lane < 96, r, pltpu.roll(r, 7, x.ndim - 2))


def y_prev(x, lane):
    r = pltpu.roll(x, 32, x.ndim - 1)
    return jnp.where(lane >= 32, r, pltpu.roll(r, 1, x.ndim - 2))


def z_next(x):
    return pltpu.roll(x, 127, x.ndim - 1)


def z_prev(x):
    return pltpu.roll(x, 1, x.ndim - 1)


def kernel(
    n,
    counts_hbm,
    resid_hbm,
    accum_hbm,
    mobility_hbm,
    trans_hbm,
    decouple_hbm,
    out,
    counts,
    resid,
    accum,
    mobility,
    trans,
    decouple,
    own,
    pown,
    below1,
    above1,
    below2,
    above2,
    fup,
    fbelow,
    fabove,
    pw,
    coef,
    direction,
    remain,
    total,
    fine,
    blocks,
    carried,
    target,
    result,
    send_sem,
    recv_sem,
    load_sem,
):
    me = lax.axis_index("gx")
    pairs = [
        (counts_hbm, counts),
        (mobility_hbm, mobility),
        (accum_hbm, accum),
        (resid_hbm, resid),
        (trans_hbm, trans),
        (decouple_hbm, decouple),
    ]
    loads = [
        pltpu.make_async_copy(src, dst, load_sem.at[i]) for i, (src, dst) in enumerate(pairs)
    ]
    for load in loads:
        load.start()
    grid = CX * n
    barrier = pltpu.get_barrier_semaphore()
    here = {}
    for step in (-2, -1, 1, 2):
        here[step] = (me + step >= 0) & (me + step < n)

        @pl.when(here[step])
        def _():
            pl.semaphore_signal(
                barrier, inc=1, device_id={"gx": me + step}, device_id_type=pl.DeviceIdType.MESH
            )

    loads[0].wait()
    start = jnp.int32(0)
    for part in range(n):
        start = start + jnp.where(part < me, counts[part], 0)
    count = counts[me]
    end = start + count
    base = CX * me
    drift = jnp.clip(start - base, -2, 2)
    drift_end = jnp.clip(end - base - CX, -2, 2)

    shape = (1, 8, 128)
    lane = lax.broadcasted_iota(jnp.int32, shape, 2)
    row = lax.broadcasted_iota(jnp.int32, shape, 1)
    keep_row = jnp.where((row < 7) | (lane < 96), 1.0, 0.0)
    keep_lane = jnp.where(lane % NZ < NZ - 1, 1.0, 0.0)

    def planes(first, length):
        return first + lax.broadcasted_iota(jnp.int32, (length, 8, 128), 0)

    blank = jnp.zeros((LEAD, 8, 128), jnp.float32)
    columns = (0, 3, 6, 1, 2, 4, 5, 7, 8)
    place_of = {c: i for i, c in enumerate(columns)}

    def place(i, ref, at):
        own[i, :LEAD] = blank
        own[i, LEAD:] = ref[at].reshape(CAP, 8, 128)

    for load in loads[1:]:
        load.wait()
    for i in range(3):
        place(i, mobility, 3 * i)
        place(9 + 3 * i, accum, 3 * i)
        place(18 + i, resid, i)
        place(21 + i, trans, i)
    for i in range(2):
        place(24 + i, decouple, i)

    at = 5 - drift
    spot = planes(base - 2, 12)
    mine = (spot >= start) & (spot < end)

    def field(i):
        return own[i, pl.ds(at, 12)]

    one, two = field(24), field(25)
    pown[0] = jnp.where(mine, field(18) + one * field(19) + two * field(20), 0.0)
    pown[1] = jnp.where(mine, field(0) + one * field(1) + two * field(2), 0.0)
    pown[2] = jnp.where(mine, field(9) + one * field(12) + two * field(15), 0.0)
    pown[3] = jnp.where(mine & (spot < grid - 1), field(21), 0.0)
    pown[4] = jnp.where(mine, field(22) * keep_row, 0.0)
    pown[5] = jnp.where(mine, field(23) * keep_lane, 0.0)

    for step, ref in ((-1, below1), (1, above1), (-2, below2), (2, above2)):

        @pl.when(jnp.logical_not(here[step]))
        def _():
            ref[...] = jnp.zeros_like(ref)

    known = jnp.int32(0)
    for step in here:
        known = known + here[step].astype(jnp.int32)
    pl.semaphore_wait(barrier, known)

    def send(src, dst, step, slot):
        return pltpu.make_async_remote_copy(
            src_ref=src,
            dst_ref=dst,
            send_sem=send_sem.at[slot],
            recv_sem=recv_sem.at[slot],
            device_id={"gx": me + step},
            device_id_type=pl.DeviceIdType.MESH,
        )

    copies = [
        (1, send(pown, below1, 1, 0)),
        (-1, send(pown, above1, -1, 1)),
        (2, send(pown.at[:, 7:12], below2, 2, 2)),
        (-2, send(pown.at[:, 0:5], above2, -2, 3)),
        (1, send(fup.at[0:3], fbelow.at[0:3, 4:7], 1, 4)),
        (1, send(fup.at[3:21, 1:3], fbelow.at[3:21, 5:7], 1, 5)),
        (-1, send(own.at[0:3, LEAD : LEAD + 3], fabove.at[0:3, 4:7], -1, 6)),
        (-1, send(own.at[3:21, LEAD : LEAD + 2], fabove.at[3:21, 4:6], -1, 7)),
    ]

    def start_all(some):
        for step, copy in some:

            @pl.when(here[step])
            def _():
                copy.start()

    start_all(copies[:4])
    for i in range(3):
        for c in (1, 2):
            place(place_of[3 * i + c], mobility, 3 * i + c)
            place(9 + 3 * i + c, accum, 3 * i + c)
    for i in range(21):
        fup[i] = own[i, pl.ds(LEAD + jnp.clip(count, 4, 12) - 3, 3)]
    start_all(copies[4:])

    for step, copy in copies[:4]:

        @pl.when(here[-step])
        def _():
            copy.wait_recv()

    for i in range(6):
        pw[i, 0:1] = below2[i, 0:1]
        pw[i, 1:5] = below2[i, 1:5] + below1[i, 0:4]
        pw[i, 5:9] = below1[i, 4:8]
        pw[i, 9:13] = below1[i, 8:12] + pown[i, 0:4]
        pw[i, 13:17] = pown[i, 4:8]
        pw[i, 17:21] = pown[i, 8:12] + above1[i, 0:4]
        pw[i, 21:25] = above1[i, 4:8]
        pw[i, 25:29] = above1[i, 8:12] + above2[i, 0:4]
        pw[i, 29:30] = above2[i, 4:5]
    zero = jnp.zeros((1, 8, 128), jnp.float32)
    for i in range(2):
        direction[i, 0:1] = zero
        direction[i, PW - 1 : PW] = zero

    middle = 0.5 * (CHEB_HIGH + CHEB_LOW)
    radius = 0.5 * (CHEB_HIGH - CHEB_LOW)
    aspect = middle / radius
    PC = 28

    def prepare(j, _):
        k = 1 + j * PC
        lam = pw[1, pl.ds(k, PC)]
        lam_up = pw[1, pl.ds(k + 1, PC)]
        lam_down = pw[1, pl.ds(k - 1, PC)]
        tx_down = pw[3, pl.ds(k - 1, PC)]
        cx = pw[3, pl.ds(k, PC)] * (lam + lam_up) * 0.5
        cx_down = tx_down * (lam_down + lam) * 0.5
        cy = pw[4, pl.ds(k, PC)] * (lam + y_next(lam, lane)) * 0.5
        cz = pw[5, pl.ds(k, PC)] * (lam + z_next(lam)) * 0.5
        cy_down = y_prev(cy, lane)
        cz_down = z_prev(cz)
        pivot = pw[2, pl.ds(k, PC)] + cx + cx_down + cy + cy_down + cz + cz_down
        where = planes(base - 11 + k, PC)
        inverse = 1.0 / jnp.where((where >= 0) & (where < grid), pivot, 1.0)
        for i, value in enumerate((cx, cx_down, cy, cy_down, cz, cz_down)):
            coef[i, pl.ds(k, PC)] = value * inverse
        scaled = pw[0, pl.ds(k, PC)] * inverse
        remain[pl.ds(k, PC)] = scaled
        first = scaled / middle
        direction[0, pl.ds(k, PC)] = first
        total[pl.ds(k, PC)] = first
        return 0

    lax.fori_loop(0, (PW - 2) // PC, prepare, 0)

    factor = 1.0 / aspect
    for iteration in range(CHEB - 1):
        now, later = iteration % 2, (iteration + 1) % 2
        factor_next = 1.0 / (2.0 * aspect - factor)

        def advance(j, _, now=now, later=later, factor=factor, factor_next=factor_next):
            k = 1 + j * PC
            d = direction[now, pl.ds(k, PC)]
            across = coef[0, pl.ds(k, PC)] * direction[now, pl.ds(k + 1, PC)]
            across = across + coef[1, pl.ds(k, PC)] * direction[now, pl.ds(k - 1, PC)]
            across = across + coef[2, pl.ds(k, PC)] * y_next(d, lane)
            across = across + coef[3, pl.ds(k, PC)] * y_prev(d, lane)
            across = across + coef[4, pl.ds(k, PC)] * z_next(d)
            across = across + coef[5, pl.ds(k, PC)] * z_prev(d)
            e = remain[pl.ds(k, PC)] - d + across
            remain[pl.ds(k, PC)] = e
            d = (factor_next * factor) * d + (2.0 * factor_next / radius) * e
            direction[later, pl.ds(k, PC)] = d
            total[pl.ds(k, PC)] = total[pl.ds(k, PC)] + d
            return 0

        lax.fori_loop(0, (PW - 2) // PC, advance, 0)
        factor = factor_next

    for step, copy in copies[4:]:

        @pl.when(here[-step])
        def _():
            copy.wait_recv()

    at_own = 2 - drift
    at_below = 2 - drift
    at_above = 2 - drift_end
    spot_low = planes(base - 5, 7)
    spot_mid = planes(base + 2, 4)
    spot_high = planes(base + 6, 7)

    def owned(spot):
        return (spot >= start) & (spot < end)

    low_mine, mid_mine, high_mine = owned(spot_low), owned(spot_mid), owned(spot_high)
    for first, last, width in ((0, 3, 3), (3, 21, 2)):
        low_near = (spot_low >= start - width) & (spot_low < start) & (spot_low >= 0)
        high_near = (spot_high >= end) & (spot_high < end + width) & (spot_high < grid)

        def assemble(i, _, low_near=low_near, high_near=high_near):
            low = jnp.where(low_near, fbelow[i, pl.ds(at_below, 7)], 0.0)
            high = jnp.where(high_near, fabove[i, pl.ds(at_above, 7)], 0.0)
            fine[i, 0:7] = jnp.where(low_mine, own[i, pl.ds(at_own, 7)], low)
            fine[i, 7:11] = jnp.where(mid_mine, own[i, pl.ds(at_own + 7, 4)], 0.0)
            fine[i, 11:18] = jnp.where(high_mine, own[i, pl.ds(at_own + 11, 7)], high)
            return 0

        lax.fori_loop(first, last, assemble, 0)

    for i in range(3):
        for slot in range(2):
            carried[slot, i, 0:1] = zero
            carried[slot, i, FW - 1 : FW] = zero
        carried[1, i] = fine[i] * total[6 : 6 + FW]

    def across_of(slot, k, size):
        tx = pw[3, pl.ds(k + 6, size)]
        tx_down = pw[3, pl.ds(k + 5, size)]
        ty = pw[4, pl.ds(k + 6, size)]
        tz = pw[5, pl.ds(k + 6, size)]
        ty_down = y_prev(ty, lane)
        tz_down = z_prev(tz)
        sums = []
        for i in range(3):
            u = carried[slot, i, pl.ds(k, size)]
            value = tx * carried[slot, i, pl.ds(k + 1, size)]
            value = value + tx_down * carried[slot, i, pl.ds(k - 1, size)]
            value = value + ty * y_next(u, lane) + ty_down * y_prev(u, lane)
            value = value + tz * z_next(u) + tz_down * z_prev(u)
            sums.append(value)
        return sums, tx + tx_down + ty + ty_down + tz + tz_down

    def times(first, k, size, vector):
        return [
            blocks[first + 3 * i, pl.ds(k, size)] * vector[0]
            + blocks[first + 3 * i + 1, pl.ds(k, size)] * vector[1]
            + blocks[first + 3 * i + 2, pl.ds(k, size)] * vector[2]
            for i in range(3)
        ]

    SC = 16

    def invert(j, _):
        k = 1 + j * SC
        sums, faces = across_of(1, k, SC)
        m = [fine[place_of[i], pl.ds(k, SC)] for i in range(9)]
        b = [fine[9 + i, pl.ds(k, SC)] + faces * m[i] for i in range(9)]
        p = total[pl.ds(k + 6, SC)]
        where = planes(base - 5 + k, SC)
        inside = (where >= start - 2) & (where < end + 2) & (where >= 0) & (where < grid)
        goal = [
            jnp.where(inside, fine[18 + i, pl.ds(k, SC)] - b[3 * i] * p + sums[i], 0.0)
            for i in range(3)
        ]
        for i in range(3):
            target[i, pl.ds(k, SC)] = goal[i]
        cofactor = [
            b[4] * b[8] - b[5] * b[7],
            b[2] * b[7] - b[1] * b[8],
            b[1] * b[5] - b[2] * b[4],
            b[5] * b[6] - b[3] * b[8],
            b[0] * b[8] - b[2] * b[6],
            b[2] * b[3] - b[0] * b[5],
            b[3] * b[7] - b[4] * b[6],
            b[1] * b[6] - b[0] * b[7],
            b[0] * b[4] - b[1] * b[3],
        ]
        det = b[0] * cofactor[0] + b[1] * cofactor[3] + b[2] * cofactor[6]
        scale = 1.0 / jnp.where(inside, det, 1.0)
        inv = [jnp.where(inside, value * scale, 0.0) for value in cofactor]
        for i in range(3):
            value = 0.0
            for c in range(3):
                blocks[3 * i + c, pl.ds(k, SC)] = inv[3 * i + c]
                g = m[3 * i] * inv[c] + m[3 * i + 1] * inv[3 + c] + m[3 * i + 2] * inv[6 + c]
                blocks[9 + 3 * i + c, pl.ds(k, SC)] = g
                value = value + g * goal[c]
            carried[0, i, pl.ds(k, SC)] = value
        return 0

    lax.fori_loop(0, SW // SC, invert, 0)
    for i in range(3):
        carried[1, i, 0:1] = zero
        carried[1, i, FW - 1 : FW] = zero

    for sweep in range(SWEEPS - 1):
        now, later = sweep % 2, (sweep + 1) % 2

        def relax(j, _, now=now, later=later, last=sweep == SWEEPS - 2):
            k = 1 + j * SC
            sums, _ = across_of(now, k, SC)
            vector = [target[i, pl.ds(k, SC)] + sums[i] for i in range(3)]
            new = times(0 if last else 9, k, SC, vector)
            if last:
                new[0] = new[0] + total[pl.ds(k + 6, SC)]
            for i in range(3):
                if last:
                    result[i, pl.ds(k, SC)] = new[i]
                else:
                    carried[later, i, pl.ds(k, SC)] = new[i]
            return 0

        lax.fori_loop(0, SW // SC, relax, 0)

    slot_ids = planes(0, CAP)
    for i in range(3):
        value = result[i, pl.ds(drift + 5, CAP)]
        out[i] = jnp.where(slot_ids < count, value, 0.0)

    for step, copy in copies:

        @pl.when(here[step])
        def _():
            copy.wait_send()


def on_device(counts, resid, accum, mobility, trans, decouple):
    n = lax.axis_size("gx")
    f32 = jnp.float32

    def vmem(*dims):
        return pltpu.VMEM(dims + (8, 128), f32)

    value = pl.pallas_call(
        functools.partial(kernel, n),
        out_shape=jax.ShapeDtypeStruct((3, CAP, 8, 128), f32),
        in_specs=[pl.BlockSpec(memory_space=pltpu.HBM)] * 6,
        out_specs=pl.BlockSpec(memory_space=pltpu.VMEM),
        scratch_shapes=[
            pltpu.SMEM((n,), jnp.int32),
            pltpu.VMEM((3, CAP, 1024), f32),
            pltpu.VMEM((9, CAP, 1024), f32),
            pltpu.VMEM((9, CAP, 1024), f32),
            pltpu.VMEM((3, CAP, 1024), f32),
            pltpu.VMEM((2, CAP, 1024), f32),
            vmem(26, OWN),
            vmem(6, 12),
            vmem(6, 12),
            vmem(6, 12),
            vmem(6, 5),
            vmem(6, 5),
            vmem(21, 3),
            vmem(21, HALO),
            vmem(21, HALO),
            vmem(6, PW),
            vmem(6, PW),
            vmem(2, PW),
            vmem(PW),
            vmem(PW),
            vmem(21, FW),
            vmem(18, FW),
            vmem(2, 3, FW),
            vmem(3, FW),
            vmem(3, 24),
            pltpu.SemaphoreType.DMA((8,)),
            pltpu.SemaphoreType.DMA((8,)),
            pltpu.SemaphoreType.DMA((6,)),
        ],
        compiler_params=pltpu.CompilerParams(
            collective_id=0, has_side_effects=True, vmem_limit_bytes=64 * 1024 * 1024
        ),
    )(counts, resid, accum, mobility, trans, decouple)
    return value.reshape(3, CAP, 1024)


def solution(mesh):
    spec = P(None, ("groups", "gx"), None)
    return jax.shard_map(
        on_device,
        mesh=mesh,
        in_specs=(P("groups"),) + (spec,) * 5,
        out_specs=spec,
        check_vma=False,
    )
```

```python
import functools

import jax
import jax.numpy as jnp
from jax import lax
from jax.experimental import pallas as pl
from jax.experimental.pallas import tpu as pltpu
from jax.sharding import PartitionSpec as P

CX = 8
NZ = 32
CHEB = 6
SWEEPS = 6
CAP = 16
CHEB_LOW = 0.1
CHEB_HIGH = 2.0

LEAD = 8
OWN = LEAD + CAP
PW = 20
SW = 16
OW = 12


def y_next(x, lane):
    r = pltpu.roll(x, 96, x.ndim - 1)
    return jnp.where(lane < 96, r, pltpu.roll(r, 7, x.ndim - 2))


def y_prev(x, lane):
    r = pltpu.roll(x, 32, x.ndim - 1)
    return jnp.where(lane >= 32, r, pltpu.roll(r, 1, x.ndim - 2))


def z_next(x):
    return pltpu.roll(x, 127, x.ndim - 1)


def z_prev(x):
    return pltpu.roll(x, 1, x.ndim - 1)


def kernel(
    n,
    counts_hbm,
    resid_hbm,
    accum_hbm,
    mobility_hbm,
    trans_hbm,
    decouple_hbm,
    out,
    counts,
    resid,
    accum,
    mobility,
    trans,
    decouple,
    own,
    pslot,
    pup,
    pbelow,
    pabove,
    pw,
    coef,
    state,
    bup,
    bdown,
    bbelow,
    babove,
    column,
    inverse,
    gain,
    gup,
    gdown,
    gbelow,
    gabove,
    carried,
    target,
    rup,
    rdown,
    rbelow,
    rabove,
    result,
    send_sem,
    recv_sem,
    load_sem,
):
    me = lax.axis_index("gx")
    pairs = [
        (counts_hbm, counts),
        (mobility_hbm, mobility),
        (accum_hbm, accum),
        (resid_hbm, resid),
        (trans_hbm, trans),
        (decouple_hbm, decouple),
    ]
    loads = [
        pltpu.make_async_copy(src, dst, load_sem.at[i]) for i, (src, dst) in enumerate(pairs)
    ]
    for load in loads:
        load.start()
    barrier = pltpu.get_barrier_semaphore()
    here = {-1: me > 0, 1: me < n - 1}
    for step in here:

        @pl.when(here[step])
        def _():
            pl.semaphore_signal(
                barrier, inc=1, device_id={"gx": me + step}, device_id_type=pl.DeviceIdType.MESH
            )

    loads[0].wait()
    start = jnp.int32(0)
    for part in range(n):
        start = start + jnp.where(part < me, counts[part], 0)
    count = counts[me]
    end = start + count
    base = CX * me
    drift = jnp.clip(start - base, -2, 2)
    drift_end = jnp.clip(end - base - CX, -2, 2)
    tail = jnp.clip(count, 4, 12)
    low_at = 2 - drift
    high_at = 2 - drift_end

    shape = (1, 8, 128)
    lane = lax.broadcasted_iota(jnp.int32, shape, 2)
    row = lax.broadcasted_iota(jnp.int32, shape, 1)
    keep_row = jnp.where((row < 7) | (lane < 96), 1.0, 0.0)
    keep_lane = jnp.where(lane % NZ < NZ - 1, 1.0, 0.0)

    def planes(first, length):
        return first + lax.broadcasted_iota(jnp.int32, (length, 8, 128), 0)

    def tiles(value):
        return value.reshape(CAP, 8, 128)

    blank = jnp.zeros((LEAD, 8, 128), jnp.float32)
    zero = jnp.zeros((1, 8, 128), jnp.float32)
    slot_ids = planes(0, CAP)
    held = slot_ids < count

    for load in loads[1:]:
        load.wait()
    one, two = decouple[0], decouple[1]
    fields = [
        tiles(mobility[0] + one * mobility[3] + two * mobility[6]),
        jnp.where(slot_ids + start < CX * n - 1, tiles(trans[0]), 0.0),
        tiles(resid[0] + one * resid[1] + two * resid[2]),
        tiles(accum[0] + one * accum[3] + two * accum[6]),
        tiles(trans[1]) * keep_row,
        tiles(trans[2]) * keep_lane,
        tiles(mobility[0]),
        tiles(mobility[3]),
        tiles(mobility[6]),
    ]
    for i, value in enumerate(fields):
        pslot[i, :LEAD] = blank
        pslot[i, LEAD:] = jnp.where(held, value, 0.0)
    for i in range(9):
        pup[i] = pslot[i, pl.ds(LEAD + tail - 4, 4)]

    pl.semaphore_wait(barrier, here[-1].astype(jnp.int32) + here[1].astype(jnp.int32))

    def send(src, dst, step, slot):
        return pltpu.make_async_remote_copy(
            src_ref=src,
            dst_ref=dst,
            send_sem=send_sem.at[slot],
            recv_sem=recv_sem.at[slot],
            device_id={"gx": me + step},
            device_id_type=pl.DeviceIdType.MESH,
        )

    L = LEAD
    phase_a = [
        (1, send(pup.at[0:2], pbelow.at[0:2, 4:8], 1, 0)),
        (-1, send(pslot.at[0:2, L : L + 4], pabove.at[0:2, 4:8], -1, 1)),
        (1, send(pup.at[2:6, 1:4], pbelow.at[2:6, 5:8], 1, 2)),
        (-1, send(pslot.at[2:6, L : L + 3], pabove.at[2:6, 4:7], -1, 3)),
    ]
    phase_m = [
        (1, send(pup.at[6:9, 3:4], pbelow.at[6:9, 7:8], 1, 4)),
        (-1, send(pslot.at[6:9, L : L + 1], pabove.at[6:9, 4:5], -1, 5)),
    ]
    phase_b = [
        (1, send(bup, bbelow.at[:, 4:7], 1, 6)),
        (-1, send(bdown, babove.at[:, 4:7], -1, 7)),
    ]
    phase_g = [
        (1, send(gup, gbelow.at[:, 4:6], 1, 8)),
        (-1, send(gdown, gabove.at[:, 4:6], -1, 9)),
    ]
    phase_r = [
        (1, send(rup, rbelow.at[:, 4:6], 1, 10)),
        (-1, send(rdown, rabove.at[:, 4:6], -1, 11)),
    ]

    def begin(phase):
        for step, copy in phase:

            @pl.when(here[step])
            def _(copy=copy):
                copy.start()

    def arrive(phase):
        for step, copy in phase:

            @pl.when(here[-step])
            def _(copy=copy):
                copy.wait_recv()

    begin(phase_a)
    begin(phase_m)

    rest = [(mobility, 3 * i + c) for i in range(3) for c in (1, 2)]
    rest += [(accum, i) for i in range(9)] + [(resid, i) for i in range(3)]
    for i, (ref, at) in enumerate(rest):
        own[i, :LEAD] = blank
        own[i, LEAD:] = tiles(ref[at])

    arrive(phase_a)
    arrive(phase_m)

    spot_low, spot_high = planes(base - 6, 8), planes(base + 6, 8)

    def near_low(width):
        return (spot_low >= start - width) & (spot_low < start) & (spot_low >= 0)

    def near_high(width):
        return (spot_high >= end) & (spot_high < end + width) & (spot_high < CX * n)

    for i in range(9):
        width = 4 if i < 2 else 3 if i < 6 else 1
        mine = pslot[i, pl.ds(low_at, PW)]
        pw[i, 0:8] = jnp.where(near_low(width), pbelow[i, pl.ds(low_at, 8)], mine[0:8])
        pw[i, 8:12] = mine[8:12]
        pw[i, 12:20] = jnp.where(near_high(width), pabove[i, pl.ds(high_at, 8)], mine[12:20])

    middle = 0.5 * (CHEB_HIGH + CHEB_LOW)
    radius = 0.5 * (CHEB_HIGH - CHEB_LOW)
    aspect = middle / radius
    inner = slice(1, PW - 1)
    for i in range(2):
        state[i, 0:1] = zero
        state[i, PW - 1 : PW] = zero
    lam = pw[0]
    cx_all = pw[1, 0 : PW - 1] * (lam[0 : PW - 1] + lam[1:PW]) * 0.5
    cx, cx_down = cx_all[1:], cx_all[:-1]
    lam = lam[inner]
    cy = pw[4, inner] * (lam + y_next(lam, lane)) * 0.5
    cz = pw[5, inner] * (lam + z_next(lam)) * 0.5
    cy_down = y_prev(cy, lane)
    cz_down = z_prev(cz)
    pivot = pw[3, inner] + cx + cx_down + cy + cy_down + cz + cz_down
    spot = planes(base - 5, PW - 2)
    valid = (spot >= start - 3) & (spot < end + 3) & (spot >= 0) & (spot < CX * n)
    scale = 1.0 / jnp.where(valid, pivot, 1.0)
    for i, value in enumerate((cx, cx_down, cy, cy_down, cz, cz_down)):
        coef[i] = value * scale
    scaled = pw[2, inner] * scale
    state[2, inner] = scaled
    state[0, inner] = scaled / middle
    state[3, inner] = scaled / middle
    pw[9, inner] = y_prev(pw[4, inner], lane)
    pw[10, inner] = z_prev(pw[5, inner])

    def advance(iteration, factor):
        now, later = iteration % 2, (iteration + 1) % 2
        factor_next = 1.0 / (2.0 * aspect - factor)
        d = state[now, inner]
        across = coef[0] * state[now, 2:PW] + coef[1] * state[now, 0 : PW - 2]
        across = across + coef[2] * y_next(d, lane) + coef[3] * y_prev(d, lane)
        across = across + coef[4] * z_next(d) + coef[5] * z_prev(d)
        e = state[2, inner] - d + across
        state[2, inner] = e
        d = (factor_next * factor) * d + (2.0 * factor_next / radius) * e
        state[later, inner] = d
        state[3, inner] = state[3, inner] + d
        return factor_next

    factor = 1.0 / aspect
    for iteration in range(3):
        factor = advance(iteration, factor)

    for i in range(3):
        bup[i] = state[1 + i, pl.ds(11 + drift_end, 3)]
        bdown[i] = state[1 + i, pl.ds(6 + drift, 3)]
    begin(phase_b)

    spot = planes(base - 2, OW)
    mine = (spot >= start) & (spot < end)
    middle_planes = slice(4, 4 + OW)
    faces = pw[1, middle_planes] + pw[1, 3 : 3 + OW] + pw[4, middle_planes] + pw[9, middle_planes]
    faces = faces + pw[5, middle_planes] + pw[10, middle_planes]

    def block(i):
        return own[i, pl.ds(low_at + 4, OW)]

    m = []
    for i in range(3):
        m += [pw[6 + i, middle_planes], block(2 * i), block(2 * i + 1)]
    b = [block(6 + i) + faces * m[i] for i in range(9)]
    cofactor = [
        b[4] * b[8] - b[5] * b[7],
        b[2] * b[7] - b[1] * b[8],
        b[1] * b[5] - b[2] * b[4],
        b[5] * b[6] - b[3] * b[8],
        b[0] * b[8] - b[2] * b[6],
        b[2] * b[3] - b[0] * b[5],
        b[3] * b[7] - b[4] * b[6],
        b[1] * b[6] - b[0] * b[7],
        b[0] * b[4] - b[1] * b[3],
    ]
    det = b[0] * cofactor[0] + b[1] * cofactor[3] + b[2] * cofactor[6]
    scale = 1.0 / jnp.where(mine, det, 1.0)
    inv = [jnp.where(mine, value * scale, 0.0) for value in cofactor]
    edge = jnp.zeros((2, 8, 128), jnp.float32)
    for i in range(3):
        column[i] = b[3 * i]
        for c in range(3):
            inverse[3 * i + c] = inv[3 * i + c]
            value = m[3 * i] * inv[c] + m[3 * i + 1] * inv[3 + c] + m[3 * i + 2] * inv[6 + c]
            gain[3 * i + c, 0:2] = edge
            gain[3 * i + c, 2 : 2 + OW] = jnp.where(mine, value, 0.0)
            gain[3 * i + c, 2 + OW : SW] = edge
    for i in range(9):
        gup[i] = gain[i, pl.ds(10 + drift_end, 2)]
        gdown[i] = gain[i, pl.ds(4 + drift, 2)]
    begin(phase_g)

    arrive(phase_b)
    for i in range(3):
        low = jnp.where(near_low(3)[1:8], bbelow[i, pl.ds(low_at, 7)], state[1 + i, 1:8])
        high = jnp.where(near_high(3)[0:7], babove[i, pl.ds(high_at, 7)], state[1 + i, 12:19])
        state[1 + i, 1:8] = low
        state[1 + i, 12:19] = high
    for iteration in range(3, CHEB - 1):
        factor = advance(iteration, factor)

    for i in range(3):
        for slot in range(2):
            carried[slot, i, 0:1] = zero
            carried[slot, i, SW + 1 : SW + 2] = zero

    def across_of(first, u, up, down, length):
        here_planes = slice(first, first + length)
        value = pw[1, here_planes] * up + pw[1, first - 1 : first - 1 + length] * down
        value = value + pw[4, here_planes] * y_next(u, lane) + pw[9, here_planes] * y_prev(u, lane)
        return value + pw[5, here_planes] * z_next(u) + pw[10, here_planes] * z_prev(u)

    pressure = state[3, 3 : 5 + OW]
    for i in range(3):
        v = pw[6 + i, 3 : 5 + OW] * pressure
        sums = across_of(4, v[1 : 1 + OW], v[2 : 2 + OW], v[0:OW], OW)
        goal = own[15 + i, pl.ds(low_at + 4, OW)] - column[i] * pressure[1 : 1 + OW] + sums
        target[i, 0:2] = edge
        target[i, 2 : 2 + OW] = jnp.where(mine, goal, 0.0)
        target[i, 2 + OW : SW] = edge
    for i in range(3):
        rup[i] = target[i, pl.ds(10 + drift_end, 2)]
        rdown[i] = target[i, pl.ds(4 + drift, 2)]
    begin(phase_r)

    def merge(ref, i, below, above):
        low = jnp.where(near_low(2)[2:8], below[i, pl.ds(low_at, 6)], ref[i, 0:6])
        high = jnp.where(near_high(2)[0:6], above[i, pl.ds(high_at, 6)], ref[i, 10:16])
        ref[i, 0:6] = low
        ref[i, 10:16] = high

    arrive(phase_g)
    for i in range(9):
        merge(gain, i, gbelow, gabove)
    arrive(phase_r)
    for i in range(3):
        merge(target, i, rbelow, rabove)

    def times(blocks, vector):
        return [
            blocks[3 * i] * vector[0]
            + blocks[3 * i + 1] * vector[1]
            + blocks[3 * i + 2] * vector[2]
            for i in range(3)
        ]

    first = times(gain, [target[i] for i in range(3)])
    for i in range(3):
        carried[0, i, 1 : 1 + SW] = first[i]
    for sweep in range(SWEEPS - 2):
        now, later = sweep % 2, (sweep + 1) % 2
        vector = []
        for i in range(3):
            u = carried[now, i]
            sums = across_of(2, u[1 : 1 + SW], u[2 : 2 + SW], u[0:SW], SW)
            vector.append(target[i] + sums)
        new = times(gain, vector)
        for i in range(3):
            carried[later, i, 1 : 1 + SW] = new[i]
    now = (SWEEPS - 2) % 2
    vector = []
    for i in range(3):
        u = carried[now, i, 2 : 4 + OW]
        sums = across_of(4, u[1 : 1 + OW], u[2 : 2 + OW], u[0:OW], OW)
        vector.append(target[i, 2 : 2 + OW] + sums)
    new = times(inverse, vector)
    new[0] = new[0] + state[3, 4 : 4 + OW]
    for i in range(3):
        result[i, 0:OW] = new[i]
        value = result[i, pl.ds(2 + drift, CAP)]
        out[i] = jnp.where(held, value, 0.0)

    for step, copy in phase_a + phase_m + phase_b + phase_g + phase_r:

        @pl.when(here[step])
        def _(copy=copy):
            copy.wait_send()


def on_device(counts, resid, accum, mobility, trans, decouple):
    n = lax.axis_size("gx")
    f32 = jnp.float32

    def vmem(*dims):
        return pltpu.VMEM(dims + (8, 128), f32)

    raw = [pltpu.VMEM((fields, CAP, 1024), f32) for fields in (3, 9, 9, 3, 2)]
    value = pl.pallas_call(
        functools.partial(kernel, n),
        out_shape=jax.ShapeDtypeStruct((3, CAP, 8, 128), f32),
        in_specs=[pl.BlockSpec(memory_space=pltpu.HBM)] * 6,
        out_specs=pl.BlockSpec(memory_space=pltpu.VMEM),
        scratch_shapes=[pltpu.SMEM((n,), jnp.int32)]
        + raw
        + [
            vmem(18, OWN),
            vmem(9, OWN),
            vmem(9, 4),
            vmem(9, 12),
            vmem(9, 12),
            vmem(11, PW),
            vmem(6, PW - 2),
            vmem(4, PW),
            vmem(3, 3),
            vmem(3, 3),
            vmem(3, 11),
            vmem(3, 11),
            vmem(3, OW),
            vmem(9, OW),
            vmem(9, SW),
            vmem(9, 2),
            vmem(9, 2),
            vmem(9, 10),
            vmem(9, 10),
            vmem(2, 3, SW + 2),
            vmem(3, SW),
            vmem(3, 2),
            vmem(3, 2),
            vmem(3, 10),
            vmem(3, 10),
            vmem(3, 20),
            pltpu.SemaphoreType.DMA((12,)),
            pltpu.SemaphoreType.DMA((12,)),
            pltpu.SemaphoreType.DMA((6,)),
        ],
        compiler_params=pltpu.CompilerParams(
            collective_id=0, has_side_effects=True, vmem_limit_bytes=64 * 1024 * 1024
        ),
    )(counts, resid, accum, mobility, trans, decouple)
    return value.reshape(3, CAP, 1024)


def solution(mesh):
    spec = P(None, ("groups", "gx"), None)
    return jax.shard_map(
        on_device,
        mesh=mesh,
        in_specs=(P("groups"),) + (spec,) * 5,
        out_specs=spec,
        check_vma=False,
    )
```

```python
import functools

import jax
import jax.numpy as jnp
from jax import lax
from jax.experimental import pallas as pl
from jax.experimental.pallas import tpu as pltpu
from jax.sharding import PartitionSpec as P

CX = 8
NZ = 32
CHEB = 6
SWEEPS = 6
CAP = 16
CHEB_LOW = 0.1
CHEB_HIGH = 2.0

LEAD = 9
OWN = LEAD + CAP + 1
PW = 22
SW = 16
OW = 12


def y_next(x, lane):
    r = pltpu.roll(x, 96, x.ndim - 1)
    return jnp.where(lane < 96, r, pltpu.roll(r, 7, x.ndim - 2))


def y_prev(x, lane):
    r = pltpu.roll(x, 32, x.ndim - 1)
    return jnp.where(lane >= 32, r, pltpu.roll(r, 1, x.ndim - 2))


def z_next(x):
    return pltpu.roll(x, 127, x.ndim - 1)


def z_prev(x):
    return pltpu.roll(x, 1, x.ndim - 1)


def kernel(
    n,
    counts_hbm,
    resid_hbm,
    accum_hbm,
    mobility_hbm,
    trans_hbm,
    decouple_hbm,
    out,
    counts,
    resid,
    accum,
    mobility,
    trans,
    decouple,
    own,
    pslot,
    pup,
    pbelow,
    pabove,
    qbelow,
    qabove,
    mbelow,
    mabove,
    pw,
    coef,
    state,
    bup,
    bdown,
    bbelow,
    babove,
    inverse,
    gain,
    gup,
    gdown,
    gbelow,
    gabove,
    carried,
    target,
    result,
    send_sem,
    recv_sem,
    load_sem,
):
    me = lax.axis_index("gx")
    pairs = [
        (counts_hbm, counts),
        (mobility_hbm, mobility),
        (accum_hbm, accum),
        (resid_hbm, resid),
        (trans_hbm, trans),
        (decouple_hbm, decouple),
    ]
    loads = [
        pltpu.make_async_copy(src, dst, load_sem.at[i]) for i, (src, dst) in enumerate(pairs)
    ]
    for load in loads:
        load.start()
    barrier = pltpu.get_barrier_semaphore()
    here = {-2: me > 1, -1: me > 0, 1: me < n - 1, 2: me < n - 2}
    for step in here:

        @pl.when(here[step])
        def _():
            pl.semaphore_signal(
                barrier, inc=1, device_id={"gx": me + step}, device_id_type=pl.DeviceIdType.MESH
            )

    loads[0].wait()
    start = jnp.int32(0)
    for part in range(n):
        start = start + jnp.where(part < me, counts[part], 0)
    count = counts[me]
    end = start + count
    count_low = counts[jnp.maximum(me - 1, 0)]
    count_high = counts[jnp.minimum(me + 1, n - 1)]
    base = CX * me
    drift = jnp.clip(start - base, -2, 2)
    drift_end = jnp.clip(end - base - CX, -2, 2)
    tail = jnp.clip(count, 4, 12)
    low_at = 2 - drift
    high_at = 2 - drift_end

    shape = (1, 8, 128)
    lane = lax.broadcasted_iota(jnp.int32, shape, 2)
    row = lax.broadcasted_iota(jnp.int32, shape, 1)
    keep_row = jnp.where((row < 7) | (lane < 96), 1.0, 0.0)
    keep_lane = jnp.where(lane % NZ < NZ - 1, 1.0, 0.0)

    def planes(first, length):
        return first + lax.broadcasted_iota(jnp.int32, (length, 8, 128), 0)

    def tiles(value):
        return value.reshape(CAP, 8, 128)

    blank = jnp.zeros((LEAD, 8, 128), jnp.float32)
    zero = jnp.zeros((1, 8, 128), jnp.float32)
    slot_ids = planes(0, CAP)
    held = slot_ids < count

    for load in loads[1:]:
        load.wait()
    one, two = decouple[0], decouple[1]
    fields = [
        tiles(mobility[0] + one * mobility[3] + two * mobility[6]),
        jnp.where(slot_ids + start < CX * n - 1, tiles(trans[0]), 0.0),
        tiles(resid[0] + one * resid[1] + two * resid[2]),
        tiles(accum[0] + one * accum[3] + two * accum[6]),
        tiles(trans[1]) * keep_row,
        tiles(trans[2]) * keep_lane,
        tiles(mobility[0]),
        tiles(mobility[3]),
        tiles(mobility[6]),
        tiles(accum[0]),
        tiles(accum[3]),
        tiles(accum[6]),
        tiles(resid[0]),
        tiles(resid[1]),
        tiles(resid[2]),
    ]
    for i, value in enumerate(fields):
        pslot[i, :LEAD] = blank
        pslot[i, LEAD : LEAD + CAP] = jnp.where(held, value, 0.0)
        pslot[i, LEAD + CAP :] = zero
    for i in range(15):
        pup[i] = pslot[i, pl.ds(LEAD + tail - 5, 5)]

    known = jnp.int32(0)
    for step in here:
        known = known + here[step].astype(jnp.int32)
    pl.semaphore_wait(barrier, known)

    def send(src, dst, step, slot):
        return pltpu.make_async_remote_copy(
            src_ref=src,
            dst_ref=dst,
            send_sem=send_sem.at[slot],
            recv_sem=recv_sem.at[slot],
            device_id={"gx": me + step},
            device_id_type=pl.DeviceIdType.MESH,
        )

    L = LEAD
    phase_a = [
        (1, send(pup.at[0:2], pbelow.at[0:2, 4:9], 1, 0)),
        (-1, send(pslot.at[0:2, L : L + 5], pabove.at[0:2, 4:9], -1, 1)),
        (1, send(pup.at[2:6, 1:5], pbelow.at[2:6, 5:9], 1, 2)),
        (-1, send(pslot.at[2:6, L : L + 4], pabove.at[2:6, 4:8], -1, 3)),
        (2, send(pup.at[0:2, 4:5], qbelow, 2, 4)),
        (-2, send(pslot.at[0:2, L : L + 1], qabove, -2, 5)),
    ]
    phase_m = [
        (1, send(pup.at[6:9, 2:5], mbelow.at[0:3, 6:9], 1, 6)),
        (-1, send(pslot.at[6:9, L : L + 3], mabove.at[0:3, 4:7], -1, 7)),
        (1, send(pup.at[9:15, 3:5], mbelow.at[3:9, 7:9], 1, 8)),
        (-1, send(pslot.at[9:15, L : L + 2], mabove.at[3:9, 4:6], -1, 9)),
    ]
    phase_b = [
        (1, send(bup, bbelow.at[:, 4:9], 1, 10)),
        (-1, send(bdown, babove.at[:, 4:9], -1, 11)),
    ]
    phase_g = [
        (1, send(gup, gbelow.at[:, 4:6], 1, 12)),
        (-1, send(gdown, gabove.at[:, 4:6], -1, 13)),
    ]

    def begin(phase):
        for step, copy in phase:

            @pl.when(here[step])
            def _(copy=copy):
                copy.start()

    def arrive(phase):
        for step, copy in phase:

            @pl.when(here[-step])
            def _(copy=copy):
                copy.wait_recv()

    begin(phase_a)
    begin(phase_m)

    rest = [(mobility, 3 * i + c) for i in range(3) for c in (1, 2)]
    rest += [(accum, 3 * i + c) for i in range(3) for c in (1, 2)]
    for i, (ref, at) in enumerate(rest):
        own[i, :LEAD] = blank
        own[i, LEAD : LEAD + CAP] = tiles(ref[at])
        own[i, LEAD + CAP :] = zero

    arrive(phase_a)

    spot_low, spot_high = planes(base - 7, 9), planes(base + 6, 9)

    def near_low(width):
        return (spot_low >= start - width) & (spot_low < start) & (spot_low >= 0)

    def near_high(width):
        return (spot_high >= end) & (spot_high < end + width) & (spot_high < CX * n)

    def assemble(i):
        width = 5 if i < 2 else 4 if i < 6 else 3 if i < 9 else 2
        mine = pslot[i, pl.ds(low_at, PW)]
        below, above, at = (pbelow, pabove, i) if i < 6 else (mbelow, mabove, i - 6)
        low = jnp.where(near_low(width), below[at, pl.ds(low_at, 9)], mine[0:9])
        high = jnp.where(near_high(width), above[at, pl.ds(high_at, 9)], mine[13:22])
        if i < 2:
            beyond = (spot_low == start - 5) & (count_low == 4) & (spot_low >= 0)
            low = jnp.where(beyond, qbelow[i], low)
            beyond = (spot_high == end + 4) & (count_high == 4) & (spot_high < CX * n)
            high = jnp.where(beyond, qabove[i], high)
        pw[i, 0:9] = low
        pw[i, 9:13] = mine[9:13]
        pw[i, 13:22] = high

    for i in range(6):
        assemble(i)
    inner = slice(1, PW - 1)
    pw[15, inner] = y_prev(pw[4, inner], lane)
    pw[16, inner] = z_prev(pw[5, inner])

    def face_total(first, length):
        span = slice(first, first + length)
        total = pw[1, span] + pw[1, first - 1 : first - 1 + length]
        return total + pw[4, span] + pw[15, span] + pw[5, span] + pw[16, span]

    spot = planes(base - 2, OW)
    mine = (spot >= start) & (spot < end)
    faces = face_total(5, OW)

    def block(i):
        return own[i, pl.ds(low_at + 5, OW)]

    m = []
    for i in range(3):
        m += [pslot[6 + i, pl.ds(low_at + 5, OW)], block(2 * i), block(2 * i + 1)]
    a = []
    for i in range(3):
        a += [pslot[9 + i, pl.ds(low_at + 5, OW)], block(6 + 2 * i), block(7 + 2 * i)]
    b = [a[i] + faces * m[i] for i in range(9)]
    cofactor = [
        b[4] * b[8] - b[5] * b[7],
        b[2] * b[7] - b[1] * b[8],
        b[1] * b[5] - b[2] * b[4],
        b[5] * b[6] - b[3] * b[8],
        b[0] * b[8] - b[2] * b[6],
        b[2] * b[3] - b[0] * b[5],
        b[3] * b[7] - b[4] * b[6],
        b[1] * b[6] - b[0] * b[7],
        b[0] * b[4] - b[1] * b[3],
    ]
    det = b[0] * cofactor[0] + b[1] * cofactor[3] + b[2] * cofactor[6]
    scale = 1.0 / jnp.where(mine, det, 1.0)
    inv = [jnp.where(mine, value * scale, 0.0) for value in cofactor]
    edge = jnp.zeros((2, 8, 128), jnp.float32)
    for i in range(3):
        for c in range(3):
            inverse[3 * i + c] = inv[3 * i + c]
            value = m[3 * i] * inv[c] + m[3 * i + 1] * inv[3 + c] + m[3 * i + 2] * inv[6 + c]
            gain[3 * i + c, 0:2] = edge
            gain[3 * i + c, 2 : 2 + OW] = jnp.where(mine, value, 0.0)
            gain[3 * i + c, 2 + OW : SW] = edge
    for i in range(9):
        gup[i] = gain[i, pl.ds(10 + drift_end, 2)]
        gdown[i] = gain[i, pl.ds(4 + drift, 2)]
    begin(phase_g)

    middle = 0.5 * (CHEB_HIGH + CHEB_LOW)
    radius = 0.5 * (CHEB_HIGH - CHEB_LOW)
    aspect = middle / radius
    for i in range(2):
        state[i, 0:1] = zero
        state[i, PW - 1 : PW] = zero
    lam = pw[0]
    cx_all = pw[1, 0 : PW - 1] * (lam[0 : PW - 1] + lam[1:PW]) * 0.5
    cx, cx_down = cx_all[1:], cx_all[:-1]
    lam = lam[inner]
    cy = pw[4, inner] * (lam + y_next(lam, lane)) * 0.5
    cz = pw[5, inner] * (lam + z_next(lam)) * 0.5
    cy_down = y_prev(cy, lane)
    cz_down = z_prev(cz)
    pivot = pw[3, inner] + cx + cx_down + cy + cy_down + cz + cz_down
    spot = planes(base - 6, PW - 2)
    valid = (spot >= start - 4) & (spot < end + 4) & (spot >= 0) & (spot < CX * n)
    scale = 1.0 / jnp.where(valid, pivot, 1.0)
    for i, value in enumerate((cx, cx_down, cy, cy_down, cz, cz_down)):
        coef[i] = value * scale
    scaled = pw[2, inner] * scale
    state[2, inner] = scaled
    state[0, inner] = scaled / middle
    state[3, inner] = scaled / middle

    def advance(iteration, factor):
        now, later = iteration % 2, (iteration + 1) % 2
        factor_next = 1.0 / (2.0 * aspect - factor)
        d = state[now, inner]
        across = coef[0] * state[now, 2:PW] + coef[1] * state[now, 0 : PW - 2]
        across = across + coef[2] * y_next(d, lane) + coef[3] * y_prev(d, lane)
        across = across + coef[4] * z_next(d) + coef[5] * z_prev(d)
        e = state[2, inner] - d + across
        state[2, inner] = e
        d = (factor_next * factor) * d + (2.0 * factor_next / radius) * e
        state[later, inner] = d
        state[3, inner] = state[3, inner] + d
        return factor_next

    factor = 1.0 / aspect
    for iteration in range(3):
        factor = advance(iteration, factor)

    for i in range(3):
        bup[i] = state[1 + i, pl.ds(10 + drift_end, 5)]
        bdown[i] = state[1 + i, pl.ds(7 + drift, 5)]
    begin(phase_b)

    arrive(phase_m)
    for i in range(6, 15):
        assemble(i)
    span = slice(3, 3 + SW)
    faces = face_total(3, SW)
    columns = [pw[9 + i, span] + faces * pw[6 + i, span] for i in range(3)]

    arrive(phase_b)
    for i in range(3):
        low = jnp.where(near_low(5), bbelow[i, pl.ds(low_at, 9)], state[1 + i, 0:9])
        high = jnp.where(near_high(5), babove[i, pl.ds(high_at, 9)], state[1 + i, 13:22])
        state[1 + i, 0:9] = low
        state[1 + i, 13:22] = high
    for iteration in range(3, CHEB - 1):
        factor = advance(iteration, factor)

    for i in range(3):
        for slot in range(2):
            carried[slot, i, 0:1] = zero
            carried[slot, i, SW + 1 : SW + 2] = zero

    def across_of(first, u, up, down, length):
        here_planes = slice(first, first + length)
        value = pw[1, here_planes] * up + pw[1, first - 1 : first - 1 + length] * down
        value = value + pw[4, here_planes] * y_next(u, lane) + pw[15, here_planes] * y_prev(u, lane)
        return value + pw[5, here_planes] * z_next(u) + pw[16, here_planes] * z_prev(u)

    spot = planes(base - 4, SW)
    inside = (spot >= start - 2) & (spot < end + 2) & (spot >= 0) & (spot < CX * n)
    pressure = state[3, 2 : 4 + SW]
    for i in range(3):
        v = pw[6 + i, 2 : 4 + SW] * pressure
        sums = across_of(3, v[1 : 1 + SW], v[2 : 2 + SW], v[0:SW], SW)
        goal = pw[12 + i, span] - columns[i] * pressure[1 : 1 + SW] + sums
        target[i] = jnp.where(inside, goal, 0.0)

    def merge(ref, i, below, above):
        low = jnp.where(near_low(2)[3:9], below[i, pl.ds(low_at, 6)], ref[i, 0:6])
        high = jnp.where(near_high(2)[0:6], above[i, pl.ds(high_at, 6)], ref[i, 10:16])
        ref[i, 0:6] = low
        ref[i, 10:16] = high

    arrive(phase_g)
    for i in range(9):
        merge(gain, i, gbelow, gabove)

    def times(blocks, vector):
        return [
            blocks[3 * i] * vector[0]
            + blocks[3 * i + 1] * vector[1]
            + blocks[3 * i + 2] * vector[2]
            for i in range(3)
        ]

    first = times(gain, [target[i] for i in range(3)])
    for i in range(3):
        carried[0, i, 1 : 1 + SW] = first[i]
    for sweep in range(SWEEPS - 2):
        now, later = sweep % 2, (sweep + 1) % 2
        vector = []
        for i in range(3):
            u = carried[now, i]
            sums = across_of(3, u[1 : 1 + SW], u[2 : 2 + SW], u[0:SW], SW)
            vector.append(target[i] + sums)
        new = times(gain, vector)
        for i in range(3):
            carried[later, i, 1 : 1 + SW] = new[i]
    now = (SWEEPS - 2) % 2
    vector = []
    for i in range(3):
        u = carried[now, i, 2 : 4 + OW]
        sums = across_of(5, u[1 : 1 + OW], u[2 : 2 + OW], u[0:OW], OW)
        vector.append(target[i, 2 : 2 + OW] + sums)
    new = times(inverse, vector)
    new[0] = new[0] + state[3, 5 : 5 + OW]
    for i in range(3):
        result[i, 0:OW] = new[i]
        value = result[i, pl.ds(2 + drift, CAP)]
        out[i] = jnp.where(held, value, 0.0)

    for step, copy in phase_a + phase_m + phase_b + phase_g:

        @pl.when(here[step])
        def _(copy=copy):
            copy.wait_send()


def on_device(counts, resid, accum, mobility, trans, decouple):
    n = lax.axis_size("gx")
    f32 = jnp.float32

    def vmem(*dims):
        return pltpu.VMEM(dims + (8, 128), f32)

    raw = [pltpu.VMEM((fields, CAP, 1024), f32) for fields in (3, 9, 9, 3, 2)]
    value = pl.pallas_call(
        functools.partial(kernel, n),
        out_shape=jax.ShapeDtypeStruct((3, CAP, 8, 128), f32),
        in_specs=[pl.BlockSpec(memory_space=pltpu.HBM)] * 6,
        out_specs=pl.BlockSpec(memory_space=pltpu.VMEM),
        scratch_shapes=[pltpu.SMEM((n,), jnp.int32)]
        + raw
        + [
            vmem(12, OWN),
            vmem(15, OWN),
            vmem(15, 5),
            vmem(6, 13),
            vmem(6, 13),
            vmem(2, 1),
            vmem(2, 1),
            vmem(9, 13),
            vmem(9, 13),
            vmem(17, PW),
            vmem(6, PW - 2),
            vmem(4, PW),
            vmem(3, 5),
            vmem(3, 5),
            vmem(3, 13),
            vmem(3, 13),
            vmem(9, OW),
            vmem(9, SW),
            vmem(9, 2),
            vmem(9, 2),
            vmem(9, 10),
            vmem(9, 10),
            vmem(2, 3, SW + 2),
            vmem(3, SW),
            vmem(3, 20),
            pltpu.SemaphoreType.DMA((14,)),
            pltpu.SemaphoreType.DMA((14,)),
            pltpu.SemaphoreType.DMA((6,)),
        ],
        compiler_params=pltpu.CompilerParams(
            collective_id=0, has_side_effects=True, vmem_limit_bytes=64 * 1024 * 1024
        ),
    )(counts, resid, accum, mobility, trans, decouple)
    return value.reshape(3, CAP, 1024)


def solution(mesh):
    spec = P(None, ("groups", "gx"), None)
    return jax.shard_map(
        on_device,
        mesh=mesh,
        in_specs=(P("groups"),) + (spec,) * 5,
        out_specs=spec,
        check_vma=False,
    )
```

```python
import functools

import jax
import jax.numpy as jnp
from jax import lax
from jax.experimental import pallas as pl
from jax.experimental.pallas import tpu as pltpu
from jax.sharding import PartitionSpec as P

CX = 8
NZ = 32
CHEB = 6
SWEEPS = 6
CAP = 16
CHEB_LOW = 0.1
CHEB_HIGH = 2.0

LEAD = 8
OWN = LEAD + CAP
PW = 20
SW = 16
OW = 12


def y_next(x, lane):
    r = pltpu.roll(x, 96, x.ndim - 1)
    return jnp.where(lane < 96, r, pltpu.roll(r, 7, x.ndim - 2))


def y_prev(x, lane):
    r = pltpu.roll(x, 32, x.ndim - 1)
    return jnp.where(lane >= 32, r, pltpu.roll(r, 1, x.ndim - 2))


def z_next(x):
    return pltpu.roll(x, 127, x.ndim - 1)


def z_prev(x):
    return pltpu.roll(x, 1, x.ndim - 1)


def kernel(
    n,
    counts_hbm,
    resid_hbm,
    accum_hbm,
    mobility_hbm,
    trans_hbm,
    decouple_hbm,
    out,
    counts,
    resid,
    accum,
    mobility,
    trans,
    decouple,
    own,
    pslot,
    pup,
    pbelow,
    pabove,
    mbelow,
    mabove,
    pw,
    coef,
    state,
    bup,
    bdown,
    bbelow,
    babove,
    column,
    inverse,
    gain,
    gup,
    gdown,
    gbelow,
    gabove,
    carried,
    target,
    rup,
    rdown,
    rbelow,
    rabove,
    result,
    send_sem,
    recv_sem,
    load_sem,
):
    me = lax.axis_index("gx")
    pairs = [
        (counts_hbm, counts),
        (mobility_hbm, mobility),
        (accum_hbm, accum),
        (resid_hbm, resid),
        (trans_hbm, trans),
        (decouple_hbm, decouple),
    ]
    loads = [
        pltpu.make_async_copy(src, dst, load_sem.at[i]) for i, (src, dst) in enumerate(pairs)
    ]
    for load in loads:
        load.start()
    barrier = pltpu.get_barrier_semaphore()
    here = {-1: me > 0, 1: me < n - 1}
    for step in here:

        @pl.when(here[step])
        def _():
            pl.semaphore_signal(
                barrier, inc=1, device_id={"gx": me + step}, device_id_type=pl.DeviceIdType.MESH
            )

    loads[0].wait()
    start = jnp.int32(0)
    for part in range(n):
        start = start + jnp.where(part < me, counts[part], 0)
    count = counts[me]
    end = start + count
    base = CX * me
    drift = jnp.clip(start - base, -2, 2)
    drift_end = jnp.clip(end - base - CX, -2, 2)
    tail = jnp.clip(count, 4, 12)
    low_at = 2 - drift
    high_at = 2 - drift_end

    shape = (1, 8, 128)
    lane = lax.broadcasted_iota(jnp.int32, shape, 2)
    row = lax.broadcasted_iota(jnp.int32, shape, 1)
    keep_row = jnp.where((row < 7) | (lane < 96), 1.0, 0.0)
    keep_lane = jnp.where(lane % NZ < NZ - 1, 1.0, 0.0)

    def planes(first, length):
        return first + lax.broadcasted_iota(jnp.int32, (length, 8, 128), 0)

    def tiles(value):
        return value.reshape(CAP, 8, 128)

    blank = jnp.zeros((LEAD, 8, 128), jnp.float32)
    zero = jnp.zeros((1, 8, 128), jnp.float32)
    slot_ids = planes(0, CAP)
    held = slot_ids < count

    for load in loads[1:]:
        load.wait()
    one, two = decouple[0], decouple[1]
    fields = [
        tiles(mobility[0] + one * mobility[3] + two * mobility[6]),
        jnp.where(slot_ids + start < CX * n - 1, tiles(trans[0]), 0.0),
        tiles(resid[0] + one * resid[1] + two * resid[2]),
        tiles(accum[0] + one * accum[3] + two * accum[6]),
        tiles(trans[1]) * keep_row,
        tiles(trans[2]) * keep_lane,
        tiles(mobility[0]),
        tiles(mobility[3]),
        tiles(mobility[6]),
    ]
    for i, value in enumerate(fields):
        pslot[i, :LEAD] = blank
        pslot[i, LEAD:] = jnp.where(held, value, 0.0)
    for i in range(9):
        pup[i] = pslot[i, pl.ds(LEAD + tail - 4, 4)]

    pl.semaphore_wait(barrier, here[-1].astype(jnp.int32) + here[1].astype(jnp.int32))

    def send(src, dst, step, slot):
        return pltpu.make_async_remote_copy(
            src_ref=src,
            dst_ref=dst,
            send_sem=send_sem.at[slot],
            recv_sem=recv_sem.at[slot],
            device_id={"gx": me + step},
            device_id_type=pl.DeviceIdType.MESH,
        )

    L = LEAD
    phase_a = [
        (1, send(pup.at[0:2], pbelow.at[0:2, 4:8], 1, 0)),
        (-1, send(pslot.at[0:2, L : L + 4], pabove.at[0:2, 4:8], -1, 1)),
        (1, send(pup.at[2:6, 1:4], pbelow.at[2:6, 5:8], 1, 2)),
        (-1, send(pslot.at[2:6, L : L + 3], pabove.at[2:6, 4:7], -1, 3)),
    ]
    phase_m = [
        (1, send(pup.at[6:9, 3:4], mbelow.at[:, 7:8], 1, 4)),
        (-1, send(pslot.at[6:9, L : L + 1], mabove.at[:, 4:5], -1, 5)),
    ]
    phase_b = [
        (1, send(bup, bbelow.at[:, 4:7], 1, 6)),
        (-1, send(bdown, babove.at[:, 4:7], -1, 7)),
    ]
    phase_g = [
        (1, send(gup, gbelow.at[:, 4:6], 1, 8)),
        (-1, send(gdown, gabove.at[:, 4:6], -1, 9)),
    ]
    phase_r = [
        (1, send(rup, rbelow.at[:, 4:6], 1, 10)),
        (-1, send(rdown, rabove.at[:, 4:6], -1, 11)),
    ]

    def begin(phase):
        for step, copy in phase:

            @pl.when(here[step])
            def _(copy=copy):
                copy.start()

    def arrive(phase):
        for step, copy in phase:

            @pl.when(here[-step])
            def _(copy=copy):
                copy.wait_recv()

    begin(phase_a)

    rest = [(mobility, 3 * i + c) for i in range(3) for c in (1, 2)]
    rest += [(accum, i) for i in range(9)] + [(resid, i) for i in range(3)]
    for i, (ref, at) in enumerate(rest):
        own[i, :LEAD] = blank
        own[i, LEAD:] = tiles(ref[at])

    arrive(phase_a)

    spot_low, spot_high = planes(base - 6, 8), planes(base + 6, 8)

    def near_low(width):
        return (spot_low >= start - width) & (spot_low < start) & (spot_low >= 0)

    def near_high(width):
        return (spot_high >= end) & (spot_high < end + width) & (spot_high < CX * n)

    def assemble(i):
        width = 4 if i < 2 else 3 if i < 6 else 1
        below, above, at = (pbelow, pabove, i) if i < 6 else (mbelow, mabove, i - 6)
        mine = pslot[i, pl.ds(low_at, PW)]
        pw[i, 0:8] = jnp.where(near_low(width), below[at, pl.ds(low_at, 8)], mine[0:8])
        pw[i, 8:12] = mine[8:12]
        pw[i, 12:20] = jnp.where(near_high(width), above[at, pl.ds(high_at, 8)], mine[12:20])

    for i in range(6):
        assemble(i)

    middle = 0.5 * (CHEB_HIGH + CHEB_LOW)
    radius = 0.5 * (CHEB_HIGH - CHEB_LOW)
    aspect = middle / radius
    inner = slice(1, PW - 1)
    for i in range(2):
        state[i, 0:1] = zero
        state[i, PW - 1 : PW] = zero
    lam = pw[0]
    cx_all = pw[1, 0 : PW - 1] * (lam[0 : PW - 1] + lam[1:PW]) * 0.5
    cx, cx_down = cx_all[1:], cx_all[:-1]
    lam = lam[inner]
    cy = pw[4, inner] * (lam + y_next(lam, lane)) * 0.5
    cz = pw[5, inner] * (lam + z_next(lam)) * 0.5
    cy_down = y_prev(cy, lane)
    cz_down = z_prev(cz)
    pivot = pw[3, inner] + cx + cx_down + cy + cy_down + cz + cz_down
    spot = planes(base - 5, PW - 2)
    valid = (spot >= start - 3) & (spot < end + 3) & (spot >= 0) & (spot < CX * n)
    scale = 1.0 / jnp.where(valid, pivot, 1.0)
    for i, value in enumerate((cx, cx_down, cy, cy_down, cz, cz_down)):
        coef[i] = value * scale
    scaled = pw[2, inner] * scale
    state[2, inner] = scaled
    state[0, inner] = scaled / middle
    state[3, inner] = scaled / middle
    pw[9, inner] = y_prev(pw[4, inner], lane)
    pw[10, inner] = z_prev(pw[5, inner])

    def advance(iteration, factor):
        now, later = iteration % 2, (iteration + 1) % 2
        factor_next = 1.0 / (2.0 * aspect - factor)
        d = state[now, inner]
        across = coef[0] * state[now, 2:PW] + coef[1] * state[now, 0 : PW - 2]
        across = across + coef[2] * y_next(d, lane) + coef[3] * y_prev(d, lane)
        across = across + coef[4] * z_next(d) + coef[5] * z_prev(d)
        e = state[2, inner] - d + across
        state[2, inner] = e
        d = (factor_next * factor) * d + (2.0 * factor_next / radius) * e
        state[later, inner] = d
        state[3, inner] = state[3, inner] + d
        return factor_next

    factor = 1.0 / aspect
    for iteration in range(3):
        factor = advance(iteration, factor)

    for i in range(3):
        bup[i] = state[1 + i, pl.ds(11 + drift_end, 3)]
        bdown[i] = state[1 + i, pl.ds(6 + drift, 3)]
    begin(phase_b)
    begin(phase_m)

    spot = planes(base - 2, OW)
    mine = (spot >= start) & (spot < end)
    middle_planes = slice(4, 4 + OW)
    faces = pw[1, middle_planes] + pw[1, 3 : 3 + OW] + pw[4, middle_planes] + pw[9, middle_planes]
    faces = faces + pw[5, middle_planes] + pw[10, middle_planes]

    def block(i):
        return own[i, pl.ds(low_at + 4, OW)]

    m = []
    for i in range(3):
        m += [pslot[6 + i, pl.ds(low_at + 4, OW)], block(2 * i), block(2 * i + 1)]
    b = [block(6 + i) + faces * m[i] for i in range(9)]
    cofactor = [
        b[4] * b[8] - b[5] * b[7],
        b[2] * b[7] - b[1] * b[8],
        b[1] * b[5] - b[2] * b[4],
        b[5] * b[6] - b[3] * b[8],
        b[0] * b[8] - b[2] * b[6],
        b[2] * b[3] - b[0] * b[5],
        b[3] * b[7] - b[4] * b[6],
        b[1] * b[6] - b[0] * b[7],
        b[0] * b[4] - b[1] * b[3],
    ]
    det = b[0] * cofactor[0] + b[1] * cofactor[3] + b[2] * cofactor[6]
    scale = 1.0 / jnp.where(mine, det, 1.0)
    inv = [jnp.where(mine, value * scale, 0.0) for value in cofactor]
    edge = jnp.zeros((2, 8, 128), jnp.float32)
    for i in range(3):
        column[i] = b[3 * i]
        for c in range(3):
            inverse[3 * i + c] = inv[3 * i + c]
            value = m[3 * i] * inv[c] + m[3 * i + 1] * inv[3 + c] + m[3 * i + 2] * inv[6 + c]
            gain[3 * i + c, 0:2] = edge
            gain[3 * i + c, 2 : 2 + OW] = jnp.where(mine, value, 0.0)
            gain[3 * i + c, 2 + OW : SW] = edge
    for i in range(9):
        gup[i] = gain[i, pl.ds(10 + drift_end, 2)]
        gdown[i] = gain[i, pl.ds(4 + drift, 2)]
    begin(phase_g)

    arrive(phase_b)
    for i in range(3):
        low = jnp.where(near_low(3)[1:8], bbelow[i, pl.ds(low_at, 7)], state[1 + i, 1:8])
        high = jnp.where(near_high(3)[0:7], babove[i, pl.ds(high_at, 7)], state[1 + i, 12:19])
        state[1 + i, 1:8] = low
        state[1 + i, 12:19] = high
    for iteration in range(3, CHEB - 1):
        factor = advance(iteration, factor)

    arrive(phase_m)
    for i in range(6, 9):
        assemble(i)

    for i in range(3):
        for slot in range(2):
            carried[slot, i, 0:1] = zero
            carried[slot, i, SW + 1 : SW + 2] = zero

    def across_of(first, u, up, down, length):
        here_planes = slice(first, first + length)
        value = pw[1, here_planes] * up + pw[1, first - 1 : first - 1 + length] * down
        value = value + pw[4, here_planes] * y_next(u, lane) + pw[9, here_planes] * y_prev(u, lane)
        return value + pw[5, here_planes] * z_next(u) + pw[10, here_planes] * z_prev(u)

    pressure = state[3, 3 : 5 + OW]
    for i in range(3):
        v = pw[6 + i, 3 : 5 + OW] * pressure
        sums = across_of(4, v[1 : 1 + OW], v[2 : 2 + OW], v[0:OW], OW)
        goal = own[15 + i, pl.ds(low_at + 4, OW)] - column[i] * pressure[1 : 1 + OW] + sums
        target[i, 0:2] = edge
        target[i, 2 : 2 + OW] = jnp.where(mine, goal, 0.0)
        target[i, 2 + OW : SW] = edge
    for i in range(3):
        rup[i] = target[i, pl.ds(10 + drift_end, 2)]
        rdown[i] = target[i, pl.ds(4 + drift, 2)]
    begin(phase_r)

    def merge(ref, i, below, above):
        low = jnp.where(near_low(2)[2:8], below[i, pl.ds(low_at, 6)], ref[i, 0:6])
        high = jnp.where(near_high(2)[0:6], above[i, pl.ds(high_at, 6)], ref[i, 10:16])
        ref[i, 0:6] = low
        ref[i, 10:16] = high

    arrive(phase_g)
    for i in range(9):
        merge(gain, i, gbelow, gabove)
    arrive(phase_r)
    for i in range(3):
        merge(target, i, rbelow, rabove)

    def times(blocks, vector):
        return [
            blocks[3 * i] * vector[0]
            + blocks[3 * i + 1] * vector[1]
            + blocks[3 * i + 2] * vector[2]
            for i in range(3)
        ]

    first = times(gain, [target[i] for i in range(3)])
    for i in range(3):
        carried[0, i, 1 : 1 + SW] = first[i]
    for sweep in range(SWEEPS - 2):
        now, later = sweep % 2, (sweep + 1) % 2
        vector = []
        for i in range(3):
            u = carried[now, i]
            sums = across_of(2, u[1 : 1 + SW], u[2 : 2 + SW], u[0:SW], SW)
            vector.append(target[i] + sums)
        new = times(gain, vector)
        for i in range(3):
            carried[later, i, 1 : 1 + SW] = new[i]
    now = (SWEEPS - 2) % 2
    vector = []
    for i in range(3):
        u = carried[now, i, 2 : 4 + OW]
        sums = across_of(4, u[1 : 1 + OW], u[2 : 2 + OW], u[0:OW], OW)
        vector.append(target[i, 2 : 2 + OW] + sums)
    new = times(inverse, vector)
    new[0] = new[0] + state[3, 4 : 4 + OW]
    for i in range(3):
        result[i, 0:OW] = new[i]
        value = result[i, pl.ds(2 + drift, CAP)]
        out[i] = jnp.where(held, value, 0.0)

    for step, copy in phase_a + phase_m + phase_b + phase_g + phase_r:

        @pl.when(here[step])
        def _(copy=copy):
            copy.wait_send()


def on_device(counts, resid, accum, mobility, trans, decouple):
    n = lax.axis_size("gx")
    f32 = jnp.float32

    def vmem(*dims):
        return pltpu.VMEM(dims + (8, 128), f32)

    raw = [pltpu.VMEM((fields, CAP, 1024), f32) for fields in (3, 9, 9, 3, 2)]
    value = pl.pallas_call(
        functools.partial(kernel, n),
        out_shape=jax.ShapeDtypeStruct((3, CAP, 8, 128), f32),
        in_specs=[pl.BlockSpec(memory_space=pltpu.HBM)] * 6,
        out_specs=pl.BlockSpec(memory_space=pltpu.VMEM),
        scratch_shapes=[pltpu.SMEM((n,), jnp.int32)]
        + raw
        + [
            vmem(18, OWN),
            vmem(9, OWN),
            vmem(9, 4),
            vmem(6, 12),
            vmem(6, 12),
            vmem(3, 12),
            vmem(3, 12),
            vmem(11, PW),
            vmem(6, PW - 2),
            vmem(4, PW),
            vmem(3, 3),
            vmem(3, 3),
            vmem(3, 11),
            vmem(3, 11),
            vmem(3, OW),
            vmem(9, OW),
            vmem(9, SW),
            vmem(9, 2),
            vmem(9, 2),
            vmem(9, 10),
            vmem(9, 10),
            vmem(2, 3, SW + 2),
            vmem(3, SW),
            vmem(3, 2),
            vmem(3, 2),
            vmem(3, 10),
            vmem(3, 10),
            vmem(3, 20),
            pltpu.SemaphoreType.DMA((12,)),
            pltpu.SemaphoreType.DMA((12,)),
            pltpu.SemaphoreType.DMA((6,)),
        ],
        compiler_params=pltpu.CompilerParams(
            collective_id=0, has_side_effects=True, vmem_limit_bytes=64 * 1024 * 1024
        ),
    )(counts, resid, accum, mobility, trans, decouple)
    return value.reshape(3, CAP, 1024)


def solution(mesh):
    spec = P(None, ("groups", "gx"), None)
    return jax.shard_map(
        on_device,
        mesh=mesh,
        in_specs=(P("groups"),) + (spec,) * 5,
        out_specs=spec,
        check_vma=False,
    )
```
